256 devices in a mesh: tile: 16 (over z, core), depth: 16 (over y, x).
Axes of the slice: x: 4, y: 4, z: 8, core: 2. Of those that a mesh axis runs over, the one named last changes fastest.
Arguments:
- volume: bfloat16 [1024, 256, 4096], P('depth', 'tile'), may hold values from 0 to 1
- tf_color: float32 [3, 16], replicated, may hold values from 0 to 1
- tf_opacity: float32 [16], replicated, may hold values from 0.0003 to 0.06
- light: float32 [3], replicated, may hold values from -3 to 3
- background: float32 [3], replicated, may hold values from 0 to 1
- exposure_prior: float32 [1], replicated, may hold values from 0.5 to 4
Outputs:
- mapped: float32 [2, 3, 256, 4096], P(None, None, 'tile', 'depth')
The draws below stay inside these ranges and needn't reach their ends.
All inputs are finite; a program needn't handle non-finite values.
Results may differ from the reference program's by a relative error of at most 0.00045.
Values may be sent and summed in bfloat16 or wider, within the bound.
No kernel may reach another device: no remote copies, remote signals or barrier semaphores. Data moves between devices by JAX's collectives and lax.ppermute only.
A program may use at most 128 MiB of HBM per device.

```python
import math
import jax
import jax.numpy as jnp
from jax import lax

W = 4096
KNOTS = 16
BINS = 64
H = 256
NZ = 1024


MODE_COUNT = 8


SHORT_WAVE = 24.0


LONG_WAVE = 480.0


def draw_volume(key, part):
    key = jax.random.fold_in(key, 7)
    mode_key = jax.random.fold_in(key, 1)
    phase_key = jax.random.fold_in(key, 2)
    noise_key = jax.random.fold_in(key, 3)
    large_amp = 0.12

    def rough_plane(plane_key):
        return jax.random.uniform(plane_key, (H, W), jnp.float32)
    spans = jax.random.uniform(mode_key, (MODE_COUNT, 3), jnp.float32)
    lengths = jnp.exp(math.log(SHORT_WAVE) + spans * (math.log(LONG_WAVE) - math.log(SHORT_WAVE)))
    waves = 6.283185307 / lengths
    phases = jax.random.uniform(phase_key, (MODE_COUNT, 3), jnp.float32) * 6.283185307
    mean_span = (spans[:, 0] + spans[:, 1] + spans[:, 2]) / 3.0
    amps = large_amp * jnp.exp((mean_span - 0.5) * (math.log(LONG_WAVE) - math.log(SHORT_WAVE)) / 3.0)
    row_pos = jnp.arange(H, dtype=jnp.float32)
    col_pos = jnp.arange(W, dtype=jnp.float32)
    row_waves = jnp.cos(waves[:, 1][:, None] * row_pos[None, :] + phases[:, 1][:, None])
    col_waves = jnp.cos(waves[:, 2][:, None] * col_pos[None, :] + phases[:, 2][:, None])
    row_ramp = 0.35 + 0.65 * row_pos / (H - 1)

    def plane_at(index):
        depth_pos = index.astype(jnp.float32)
        rough = rough_plane(jax.random.fold_in(noise_key, index))
        rough = rough + jnp.roll(rough, 1, 0) + jnp.roll(rough, -1, 0)
        rough = rough + jnp.roll(rough, 1, 1) + jnp.roll(rough, -1, 1)
        small = (rough / 9.0 - 0.5) * 3.0
        large = jnp.zeros((H, W), jnp.float32)
        for mode in range(MODE_COUNT):
            factor = amps[mode] * jnp.cos(waves[mode, 0] * depth_pos + phases[mode, 0])
            large = large + factor * (row_waves[mode][:, None] * col_waves[mode][None, :])
        density = jnp.clip(0.5 + large + small, 0.0, 1.0) * row_ramp[:, None]
        return density.astype(jnp.bfloat16)
    return lax.map(plane_at, jnp.arange(NZ, dtype=jnp.int32))


def draw_tf_opacity(key, part):
    key = jax.random.fold_in(key, 11)
    spread = jax.random.uniform(key, (KNOTS,), jnp.float32, math.log(0.6), math.log(1.2))
    position = jnp.arange(KNOTS, dtype=jnp.float32) / (KNOTS - 1)
    return 0.0005 * jnp.exp(spread + math.log(100.0) * position * position)


def bell_draw(own_key, dims, scale, most, kind=jnp.bfloat16):
    return jnp.clip(scale * jax.random.normal(own_key, dims, jnp.float32), -most, most).astype(kind)


def setup_inputs(seed: int = 0) -> dict:
    key_of = jax.random.split(jax.random.key(seed), 7)
    return {
        "volume": draw_volume(jax.random.fold_in(key_of[6], 71), 0),
        "tf_color": jnp.clip(jax.random.uniform(key_of[1], (3, KNOTS), jnp.float32, 0.0, 1.0), 0.0, 1.0),
        "tf_opacity": draw_tf_opacity(jax.random.fold_in(key_of[6], 71), 0),
        "light": bell_draw(key_of[3], (3,), 1.0, 3.0, jnp.float32),
        "background": jnp.clip(jax.random.uniform(key_of[4], (3,), jnp.float32, 0.0, 1.0), 0.0, 1.0),
        "exposure_prior": jnp.clip(jnp.exp(jax.random.uniform(key_of[5], (1,), jnp.float32, math.log(0.5), math.log(4.0))), 0.5, 4.0),
    }


AMBIENT = 0.3
GRAD_FLOOR = 0.04
REF_DEPTH = 1024.0
LUMA_EPS = 0.01
LOG_LOW = math.log(0.01)
LOG_HIGH = 0.05
EXPOSURE_KEY = 0.25

def sample_plane(below, centre_rows, above, tf_color, tf_opacity, light, step_len):
    centre = centre_rows[1:-1]
    grad_depth = 0.5 * (above[1:-1] - below[1:-1])
    grad_rows = 0.5 * (centre_rows[2:] - centre_rows[:-2])
    sided = jnp.pad(centre, ((0, 0), (1, 1)))
    grad_cols = 0.5 * (sided[:, 2:] - sided[:, :-2])
    length = jnp.sqrt(grad_depth * grad_depth + grad_rows * grad_rows + grad_cols * grad_cols + GRAD_FLOOR)
    light_len = jnp.sqrt(jnp.sum(light * light) + 1.0)
    facing = (grad_depth * light[0] + grad_rows * light[1] + grad_cols * light[2]) / (length * light_len)
    shade = AMBIENT + (1.0 - AMBIENT) * (0.5 + 0.5 * facing)
    knot_count = tf_color.shape[1]
    scaled = centre * (knot_count - 1)
    colour = jnp.zeros((3,) + centre.shape, jnp.float32)
    opacity = jnp.zeros(centre.shape, jnp.float32)
    for knot in range(knot_count):
        weight = jnp.maximum(0.0, 1.0 - jnp.abs(scaled - knot))
        colour = colour + weight[None] * tf_color[:, knot][:, None, None]
        opacity = opacity + weight * tf_opacity[knot]
    return (colour * shade[None], opacity * step_len)

def march_step(state, colour, alpha):
    front_image, back_image = state
    sample = jnp.concatenate([colour * alpha[None], alpha[None]], 0)
    front_image = front_image + (1.0 - front_image[3:4]) * sample
    back_image = sample + (1.0 - alpha[None]) * back_image
    return (front_image, back_image)

def flatten(final, background):
    return final[:3] + (1.0 - final[3:4]) * background[:, None, None]

def luma_log(colour_rgb):
    return jnp.log(0.2126 * colour_rgb[0] + 0.7152 * colour_rgb[1] + 0.0722 * colour_rgb[2] + LUMA_EPS)

def bin_centres(count):
    return LOG_LOW + jnp.arange(count, dtype=jnp.float32) * ((LOG_HIGH - LOG_LOW) / (count - 1))

def histogram(log_luma, count):
    bin_width = (LOG_HIGH - LOG_LOW) / (count - 1)
    centres = bin_centres(count)
    totals = []
    for index in range(count):
        totals.append(jnp.sum(jnp.maximum(0.0, 1.0 - jnp.abs(log_luma - centres[index]) / bin_width)))
    return jnp.stack(totals)

def tone(colour_rgb, exposure):
    scaled = exposure * colour_rgb
    return scaled / (1.0 + scaled)

def reference(volume, tf_color, tf_opacity, light, background, exposure_prior):
    depth_count, height, width = volume.shape
    step_len = REF_DEPTH / depth_count

    def plane_at(index):
        plane = lax.dynamic_index_in_dim(volume, index, 0, keepdims=False).astype(jnp.float32)
        return jnp.pad(plane, ((1, 1), (0, 0)))

    def advance(state, plane_index):
        below = plane_at(jnp.maximum(plane_index - 1, 0)) * (plane_index > 0).astype(jnp.float32)
        above = plane_at(jnp.minimum(plane_index + 1, depth_count - 1)) * (plane_index < depth_count - 1).astype(jnp.float32)
        here = plane_at(plane_index)
        colour, alpha = sample_plane(below, here, above, tf_color, tf_opacity, light, step_len)
        return (march_step(state, colour, alpha), None)
    empty = jnp.zeros((4, height, width), jnp.float32)
    (front_image, back_image), unused = lax.scan(advance, (empty, empty), jnp.arange(depth_count, dtype=jnp.int32))
    first_rgb = flatten(front_image, background)
    second_rgb = flatten(back_image, background)
    counts = histogram(luma_log(first_rgb), BINS)
    mean_log = jnp.sum(counts * bin_centres(BINS)) / (height * width)
    exposure_next = EXPOSURE_KEY * jnp.exp(-mean_log)
    return jnp.stack([tone(first_rgb, exposure_prior[0]), tone(second_rgb, exposure_next)])
```

```python
import functools
import math

import jax
import jax.numpy as jnp
import numpy as np
from jax import lax
from jax.experimental import pallas as pl
from jax.experimental.pallas import tpu as pltpu
from jax.sharding import PartitionSpec as P

f32 = jnp.float32
bf16 = jnp.bfloat16

BINS = 64
AMBIENT = 0.3
LUMA_EPS = 0.01
LOG_LOW = math.log(0.01)
LOG_HIGH = 0.05
EXPOSURE_KEY = 0.25
BIN_WIDTH = (LOG_HIGH - LOG_LOW) / (BINS - 1)

PLANES = 64
ROWS = 16
LANES = 128
DEPTH = 16
BLOCKS = 32
CHUNKS = 2
VMEM = 40 * 1024 * 1024


def segment_tables(tf_color, tf_opacity):
    f = jnp.concatenate([tf_opacity[None], tf_color], 0)
    f = jnp.concatenate([f, f[:, 15:]], 1)
    lo, mid, hi = f[:, 0:16:2], f[:, 1:16:2], f[:, 2:17:2]
    centre = (2.0 * jnp.arange(8, dtype=f32) + 1.0)[None]
    t = jnp.concatenate([mid, 0.5 * (hi - lo), 0.5 * (hi + lo) - mid, centre], 0)
    return jnp.broadcast_to(t.reshape(104, 1), (104, LANES))


def difference_matrices():
    sx = np.zeros((3, 384, LANES), np.float32)
    for variant in range(3):
        for i in range(LANES):
            if not (variant == 0 and i == 0):
                sx[variant, LANES + i - 1, i] = -1
            if not (variant == 2 and i == LANES - 1):
                sx[variant, LANES + i + 1, i] = 1
    sy = np.zeros((256, 384), np.float32)
    for p in range(16):
        for r in range(16):
            o = 16 * p + r
            sy[o, o - 1 if r > 0 else 256 + p] = -1
            sy[o, o + 1 if r < 15 else 272 + p] = 1
    return jnp.asarray(sx, bf16), jnp.asarray(sy, bf16)


def pick(table, index):
    return jnp.take_along_axis(table, index, axis=0, mode="promise_in_bounds")


def halves(x):
    x = x.astype(f32)
    return [x[0:8], x[8:16]]


def march_kernel(
    lp_ref, t_ref, sx_ref, sy_ref, vp_ref, v_ref, vn_ref, zlo_ref, zhi_ref, ylo_ref, yhi_ref,
    o_ref, dx_scr, dy_scr,
):
    lz, ly, lx = lp_ref[0], lp_ref[1], lp_ref[2]
    for g in range(4):
        s = slice(16 * g, 16 * g + 16)
        o = slice(256 * g, 256 * g + 256)
        wide = jnp.concatenate([r[s].reshape(256, LANES) for r in (vp_ref, v_ref, vn_ref)], axis=1)
        dx_scr[o] = jnp.dot(wide, sx_ref[0], preferred_element_type=f32)
        tall = jnp.concatenate(
            [v_ref[s].reshape(256, LANES), ylo_ref[s], yhi_ref[s], jnp.zeros((96, LANES), bf16)],
            axis=0,
        )
        dy_scr[o] = jnp.dot(sy_ref[...], tall, preferred_element_type=f32)
    tb = [t_ref[8 * k : 8 * k + 8, :] for k in range(13)]

    def plane(z, carry, above):
        below, here, front, through, back = carry
        new_front, new_through, new_back = [], [], []
        for h in range(2):
            v = here[h]
            rows = pl.ds(pl.multiple_of(16 * z + 8 * h, 8), 8)
            dz = above[h] - below[h]
            dx = dx_scr[rows, :]
            dy = dy_scr[rows, :]
            q = (dz * dz + 0.16) + (dy * dy + dx * dx)
            dot = (dz * lz + dy * ly) + dx * lx
            shade = 0.65 + dot * lax.rsqrt(q)
            j = (v * 7.5).astype(jnp.int32)
            u = v * 15.0 - pick(tb[12], j)
            au = jnp.abs(u)
            alpha, red, green, blue = [
                pick(tb[k], j) + pick(tb[4 + k], j) * u + pick(tb[8 + k], j) * au for k in range(4)
            ]
            w = alpha * shade
            keep = 1.0 - alpha
            p = [w * c for c in (red, green, blue)]
            new_front.append([front[h][i] + through[h] * p[i] for i in range(3)])
            new_back.append([back[h][i] * keep + p[i] for i in range(3)])
            new_through.append(through[h] * keep)
        return (here, above, new_front, new_through, new_back)

    zero = jnp.zeros((8, LANES), f32)
    one = jnp.ones((8, LANES), f32)
    carry = (halves(zlo_ref[...]), halves(v_ref[0]), [[zero] * 3] * 2, [one] * 2, [[zero] * 3] * 2)
    carry = lax.fori_loop(
        0, PLANES - 1, lambda z, c: plane(z, c, halves(v_ref[z + 1])), carry, unroll=3
    )
    carry = plane(PLANES - 1, carry, halves(zhi_ref[...]))
    _, _, front, through, back = carry
    for h in range(2):
        s = slice(8 * h, 8 * h + 8)
        for i in range(3):
            o_ref[0, i, s] = front[h][i]
            o_ref[0, 4 + i, s] = back[h][i]
        o_ref[0, 3, s] = through[h]


def march(chunk, vol, zlo, zhi, ylo, yhi, lp, tab, sx, sy):
    def block(shift):
        return pl.BlockSpec(
            (PLANES, ROWS, LANES), lambda d: (0, 0, jnp.clip(2 * d + chunk + shift, 0, BLOCKS - 1))
        )

    def edge(n):
        return pl.BlockSpec((n, LANES), lambda d: (0, 2 * d + chunk))

    def variant(d):
        at = 2 * d + chunk
        return (jnp.where(at == 0, 0, jnp.where(at == BLOCKS - 1, 2, 1)), 0, 0)

    return pl.pallas_call(
        march_kernel,
        grid=(DEPTH,),
        in_specs=[
            pl.BlockSpec(memory_space=pltpu.SMEM),
            pl.BlockSpec(tab.shape, lambda d: (0, 0)),
            pl.BlockSpec((1, 384, LANES), variant),
            pl.BlockSpec(sy.shape, lambda d: (0, 0)),
            block(-1),
            block(0),
            block(1),
            edge(ROWS),
            edge(ROWS),
            edge(PLANES),
            edge(PLANES),
        ],
        out_specs=pl.BlockSpec((1, 7, ROWS, LANES), lambda d: (d, 0, 0, 0)),
        out_shape=jax.ShapeDtypeStruct((DEPTH, 7, ROWS, LANES), f32),
        scratch_shapes=[pltpu.VMEM((1024, LANES), f32), pltpu.VMEM((1024, LANES), f32)],
        compiler_params=pltpu.CompilerParams(vmem_limit_bytes=VMEM),
        cost_estimate=pl.CostEstimate(
            flops=200_000_000, bytes_accessed=12_000_000, transcendentals=2_000_000
        ),
        name="march",
    )(lp, tab, sx, sy, vol, vol, vol, zlo, zhi, ylo, yhi)


def composite_kernel(bg_ref, prior_ref, s0_ref, s1_ref, mapped_ref, second_ref, lum_ref):
    total = jnp.zeros((8, LANES), f32)
    for c, s_ref in enumerate((s0_ref, s1_ref)):
        cols = slice(LANES * c, LANES * c + LANES)
        through = s_ref[0, 3]
        front = [s_ref[0, i] for i in range(3)]
        back = [s_ref[0, 4 + i] for i in range(3)]
        for d in range(1, DEPTH):
            t = s_ref[d, 3]
            front = [front[i] + through * s_ref[d, i] for i in range(3)]
            back = [s_ref[d, 4 + i] + t * back[i] for i in range(3)]
            through = through * t
        front = [front[i] + through * bg_ref[i] for i in range(3)]
        back = [back[i] + through * bg_ref[i] for i in range(3)]
        lum = jnp.log(0.2126 * front[0] + 0.7152 * front[1] + 0.0722 * front[2] + LUMA_EPS)
        near = jnp.clip(lum, LOG_LOW, LOG_HIGH)
        term = near * jnp.maximum(0.0, 1.0 - jnp.abs(lum - near) * (1.0 / BIN_WIDTH))
        total = total + term[0:8] + term[8:16]
        for i in range(3):
            scaled = prior_ref[0] * front[i]
            mapped_ref[i, :, cols] = scaled / (1.0 + scaled)
            second_ref[i, :, cols] = back[i]
    lum_ref[...] = jnp.sum(total, axis=0, keepdims=True)


def finish_kernel(pixels, lum_ref, mapped_ref, second_ref, o_ref):
    mean = jnp.sum(lum_ref[...], axis=(0, 1), keepdims=True) / pixels
    exposure = EXPOSURE_KEY * jnp.exp(-mean)
    for i in range(3):
        o_ref[0, i] = mapped_ref[i]
        scaled = exposure * second_ref[i]
        o_ref[1, i] = scaled / (1.0 + scaled)


def neighbours(low_source, high_source, axis):
    count = lax.axis_size(axis)
    forward = [(i, i + 1) for i in range(count - 1)]
    backward = [(target, source) for source, target in forward]
    return lax.ppermute(low_source, axis, forward), lax.ppermute(high_source, axis, backward)


def local(volume, tf_color, tf_opacity, light, background, exposure_prior):
    zlo, zhi = neighbours(volume[PLANES - 1], volume[0], "depth")
    ylo, yhi = neighbours(volume[:, ROWS - 1], volume[:, 0], "tile")
    tab = segment_tables(tf_color, tf_opacity)
    lp = (0.5 * (1.0 - AMBIENT)) * light / jnp.sqrt(jnp.sum(light * light) + 1.0)
    sx, sy = difference_matrices()
    stacks = []
    for chunk in range(CHUNKS):
        part = march(chunk, volume, zlo, zhi, ylo, yhi, lp, tab, sx, sy)
        stacks.append(lax.all_to_all(part, "depth", split_axis=0, concat_axis=0, tiled=True))
    smem = pl.BlockSpec(memory_space=pltpu.SMEM)
    vmem = pl.BlockSpec(memory_space=pltpu.VMEM)
    mapped, second, lum = pl.pallas_call(
        composite_kernel,
        in_specs=[smem, smem, vmem, vmem],
        out_specs=[vmem] * 3,
        out_shape=[
            jax.ShapeDtypeStruct((3, ROWS, 256), f32),
            jax.ShapeDtypeStruct((3, ROWS, 256), f32),
            jax.ShapeDtypeStruct((1, LANES), f32),
        ],
        name="composite",
    )(background, exposure_prior, *stacks)
    sums = lax.all_gather(lum, ("tile", "depth"), axis=0, tiled=True)
    pixels = ROWS * lax.axis_size("tile") * volume.shape[2]
    return pl.pallas_call(
        functools.partial(finish_kernel, float(pixels)),
        in_specs=[vmem] * 3,
        out_specs=vmem,
        out_shape=jax.ShapeDtypeStruct((2, 3, ROWS, 256), f32),
        name="finish",
    )(sums, mapped, second)


def solution(mesh):
    placed = (P("depth", "tile", None), P(), P(), P(), P(), P())
    return jax.shard_map(
        local, mesh=mesh, in_specs=placed, out_specs=P(None, None, "tile", "depth"), check_vma=False
    )
```

```python
import functools
import math

import jax
import jax.numpy as jnp
import numpy as np
from jax import lax
from jax.experimental import pallas as pl
from jax.experimental.pallas import tpu as pltpu
from jax.sharding import PartitionSpec as P

f32 = jnp.float32
bf16 = jnp.bfloat16

BINS = 64
AMBIENT = 0.3
LUMA_EPS = 0.01
LOG_LOW = math.log(0.01)
LOG_HIGH = 0.05
EXPOSURE_KEY = 0.25
BIN_WIDTH = (LOG_HIGH - LOG_LOW) / (BINS - 1)

PLANES = 64
ROWS = 16
LANES = 128
DEPTH = 16
WIDE = 256
KNOTS = 16
VMEM = 58 * 1024 * 1024


def difference_matrices():
    base = np.zeros((512, WIDE), np.float32)
    for i in range(WIDE):
        base[LANES + i - 1, i] = -1
        base[LANES + i + 1, i] = 1
    first = base.copy()
    first[:LANES] = 0
    last = base.copy()
    last[LANES + WIDE :] = 0
    sy = np.zeros((2, 128, WIDE), np.float32)
    for e in range(2):
        for p in range(8):
            for r in range(ROWS):
                o = ROWS * p + r
                sy[e, o, o - 1 if r > 0 else 128 + 8 * e + p] = -1
                sy[e, o, o + 1 if r < ROWS - 1 else 144 + 8 * e + p] = 1
    return jnp.asarray(np.stack([first, base, last]), bf16), jnp.asarray(sy, bf16)


def pick(table, index):
    return jnp.take_along_axis(table, index, axis=0, mode="promise_in_bounds")


def halves(x):
    x = x.astype(f32)
    return [x[0:8], x[8:16]]


def march_kernel(
    light_ref, color_ref, opacity_ref, sxf_ref, sx_ref, sxl_ref, sy_ref,
    before_ref, cur_ref, next_ref, after_ref,
    zlo_ref, zhi_ref, ylo_ref, yhi_ref, ylon_ref, yhin_ref,
    front_ref, back_ref, dxa, dya, dxb, dyb, acc, table,
):
    s = pl.program_id(0)
    squares = light_ref[0] * light_ref[0] + light_ref[1] * light_ref[1] + light_ref[2] * light_ref[2]
    scale = (0.5 * (1.0 - AMBIENT)) * lax.rsqrt(jnp.full((8, LANES), squares + 1.0, f32))
    lz, ly, lx = light_ref[0] * scale, light_ref[1] * scale, light_ref[2] * scale

    def differences(g, part, pieces, matrix, before, after, block, dx, dy):
        ref, cols = block
        planes = pl.ds(pl.multiple_of(16 * g, 16), 16)
        if part == 0:
            wide = jnp.concatenate(
                [r[planes, :, c].reshape(256, c.stop - c.start) for r, c in pieces], axis=1
            )
            rows = pl.ds(pl.multiple_of(256 * g, 256), 256)
            dx[rows, :] = jnp.dot(wide, matrix[...], preferred_element_type=f32)
        else:
            edges = [r[planes, c] for r, c in (before, after)]
            fill = jnp.zeros((96, WIDE), bf16)
            for e in range(2):
                some = pl.ds(pl.multiple_of(16 * g + 8 * e, 8), 8)
                rows = pl.ds(pl.multiple_of(256 * g + 128 * e, 128), 128)
                tall = jnp.concatenate([ref[some, :, cols].reshape(128, WIDE), *edges, fill], axis=0)
                dy[rows, :] = jnp.dot(sy_ref[e], tall, preferred_element_type=f32)

    low, high = slice(0, WIDE), slice(WIDE, 2 * WIDE)
    first = (
        [(before_ref, slice(0, 128)), (cur_ref, slice(0, 384))],
        sxf_ref, (ylo_ref, low), (yhi_ref, low), (cur_ref, low), dxa, dya,
    )
    odd = (
        [(cur_ref, slice(128, 512)), (next_ref, slice(0, 128))],
        sxl_ref, (ylo_ref, high), (yhi_ref, high), (cur_ref, high), dxb, dyb,
    )
    even = (
        [(cur_ref, slice(384, 512)), (next_ref, low), (after_ref, slice(0, 128))],
        sx_ref, (ylon_ref, low), (yhin_ref, low), (next_ref, low), dxa, dya,
    )

    @pl.when(s == 0)
    def _():
        for k in range(4):
            f = [color_ref[k - 1, i] if k else opacity_ref[i] for i in range(KNOTS)]
            for j in range(8):
                mid = f[2 * j + 1]
                rise = f[2 * j + 2] - mid if j < 7 else 0.0
                for row, value in ((k, mid), (4 + k, mid - f[2 * j]), (8 + k, rise)):
                    table[8 * row + j : 8 * row + j + 1, :] = jnp.full((1, LANES), value, f32)
        for j in range(8):
            table[96 + j : 97 + j, :] = jnp.full((1, LANES), 2.0 * j + 1.0, f32)
        for g in range(4):
            for part in range(2):
                differences(g, part, *first)

    tb = [table[8 * k : 8 * k + 8, :] for k in range(13)]

    def sample(below, v, above, dx, dy, state):
        dz = above - below
        q = (dz * dz + 0.16) + (dy * dy + dx * dx)
        dot = (dz * lz + dy * ly) + dx * lx
        shade = (AMBIENT + 0.5 * (1.0 - AMBIENT)) + dot * lax.rsqrt(q)
        j = (v * 7.5).astype(jnp.int32)
        u = v * 15.0 - pick(tb[12], j)
        left = u < 0.0
        alpha, red, green, blue = [
            pick(tb[k], j) + jnp.where(left, pick(tb[4 + k], j), pick(tb[8 + k], j)) * u
            for k in range(4)
        ]
        w = alpha * shade
        keep = 1.0 - alpha
        p = [w * c for c in (red, green, blue)]
        through = state[3]
        return (
            [state[i] + through * p[i] for i in range(3)]
            + [through * keep]
            + [state[4 + i] * keep + p[i] for i in range(3)]
        )

    for half, (dx, dy, following) in enumerate(((dxa, dya, odd), (dxb, dyb, even))):
        for side in range(2):
            for h in range(2):
                for i in range(7):
                    acc[side, h, i] = jnp.full((8, LANES), 1.0 if i == 3 else 0.0, f32)

        def group(g, unused, half=half, dx=dx, dy=dy, following=following):
            for side in range(2):
                differences(g, side, *following)
                lanes = slice(LANES * side, LANES * side + LANES)
                at = WIDE * half + LANES * side
                cols = slice(at, at + LANES)
                lo = jnp.where(g == 0, zlo_ref[:, cols], cur_ref[jnp.maximum(16 * g - 1, 0), :, cols])
                hi = jnp.where(
                    g == 3, zhi_ref[:, cols], cur_ref[jnp.minimum(16 * g + 16, PLANES - 1), :, cols]
                )
                below, here = halves(lo), halves(cur_ref[16 * g, :, cols])
                state = [[acc[side, h, i] for i in range(7)] for h in range(2)]
                for p in range(16):
                    above = halves(cur_ref[16 * g + p + 1, :, cols] if p < 15 else hi)
                    for h in range(2):
                        rows = pl.ds(pl.multiple_of(256 * g + 16 * p + 8 * h, 8), 8)
                        state[h] = sample(
                            below[h], here[h], above[h], dx[rows, lanes], dy[rows, lanes], state[h]
                        )
                    below, here = here, above
                for h in range(2):
                    for i in range(7):
                        acc[side, h, i] = state[h][i]
            return unused

        lax.fori_loop(0, 4, group, 0, unroll=4)
        for side in range(2):
            lanes = slice(LANES * side, LANES * side + LANES)
            for h in range(2):
                rows = slice(8 * h, 8 * h + 8)
                for i in range(3):
                    front_ref[half, i, rows, lanes] = acc[side, h, i]
                    back_ref[half, i, rows, lanes] = acc[side, h, 4 + i]
                front_ref[half, 3, rows, lanes] = 1.0 - acc[side, h, 3]


def march(vol, zlo, zhi, ylo, yhi, light, tf_color, tf_opacity):
    sx, sy = difference_matrices()
    steps = DEPTH // 2

    def follower(s):
        return jnp.minimum(2 * s + 2, DEPTH - 1)

    def block(width, place):
        return pl.BlockSpec((PLANES, ROWS, width), lambda s: (0, 0, place(s)))

    def matrix(place):
        return pl.BlockSpec((None, 512, WIDE), lambda s: (place(s), 0, 0))

    def edge(rows, width, place):
        return pl.BlockSpec((rows, width), lambda s: (0, place(s)))

    smem = pl.BlockSpec(memory_space=pltpu.SMEM)
    return pl.pallas_call(
        march_kernel,
        grid=(steps,),
        in_specs=[
            smem,
            smem,
            smem,
            matrix(lambda s: 0),
            matrix(lambda s: 1),
            matrix(lambda s: jnp.where(s == steps - 1, 2, 1)),
            pl.BlockSpec((2, 128, WIDE), lambda s: (0, 0, 0)),
            block(LANES, lambda s: 0),
            block(2 * WIDE, lambda s: s),
            block(WIDE, follower),
            block(LANES, lambda s: jnp.minimum(4 * s + 6, 2 * DEPTH - 1)),
            edge(ROWS, 2 * WIDE, lambda s: s),
            edge(ROWS, 2 * WIDE, lambda s: s),
            edge(PLANES, 2 * WIDE, lambda s: s),
            edge(PLANES, 2 * WIDE, lambda s: s),
            edge(PLANES, WIDE, follower),
            edge(PLANES, WIDE, follower),
        ],
        out_specs=[
            pl.BlockSpec((2, n, ROWS, WIDE), lambda s: (s, 0, 0, 0)) for n in (4, 3)
        ],
        out_shape=[jax.ShapeDtypeStruct((DEPTH, n, ROWS, WIDE), f32) for n in (4, 3)],
        scratch_shapes=[pltpu.VMEM((PLANES * ROWS, WIDE), f32)] * 4
        + [pltpu.VMEM((2, 2, 7, 8, LANES), f32), pltpu.VMEM((104, LANES), f32)],
        compiler_params=pltpu.CompilerParams(vmem_limit_bytes=VMEM),
        cost_estimate=pl.CostEstimate(
            flops=400_000_000, bytes_accessed=24_000_000, transcendentals=4_000_000
        ),
        name="march",
    )(
        light, tf_color, tf_opacity, sx, sx, sx, sy, vol, vol, vol, vol,
        zlo, zhi, ylo, yhi, ylo, yhi,
    )


def front_kernel(bg_ref, prior_ref, s_ref, mapped_ref, lum_ref):
    total = jnp.zeros((8, LANES), f32)
    for c in range(2):
        cols = slice(LANES * c, LANES * c + LANES)
        front = [s_ref[0, i, :, cols] for i in range(3)]
        through = 1.0 - s_ref[0, 3, :, cols]
        for d in range(1, DEPTH):
            front = [front[i] + through * s_ref[d, i, :, cols] for i in range(3)]
            through = through - through * s_ref[d, 3, :, cols]
        front = [front[i] + through * bg_ref[i] for i in range(3)]
        lum = jnp.log(0.2126 * front[0] + 0.7152 * front[1] + 0.0722 * front[2] + LUMA_EPS)
        near = jnp.clip(lum, LOG_LOW, LOG_HIGH)
        term = near * jnp.maximum(0.0, 1.0 - jnp.abs(lum - near) * (1.0 / BIN_WIDTH))
        total = total + term[0:8] + term[8:16]
        for i in range(3):
            scaled = prior_ref[0] * front[i]
            mapped_ref[i, :, cols] = scaled / (1.0 + scaled)
    lum_ref[...] = total


def back_kernel(bg_ref, f_ref, s_ref, second_ref):
    for c in range(2):
        cols = slice(LANES * c, LANES * c + LANES)
        back = [s_ref[0, i, :, cols] for i in range(3)]
        through = 1.0 - f_ref[0, 3, :, cols]
        for d in range(1, DEPTH):
            keep = 1.0 - f_ref[d, 3, :, cols]
            back = [s_ref[d, i, :, cols] + keep * back[i] for i in range(3)]
            through = through * keep
        for i in range(3):
            second_ref[i, :, cols] = back[i] + through * bg_ref[i]


def finish_kernel(pixels, lum_ref, mapped_ref, second_ref, o_ref):
    total = jnp.sum(jnp.sum(lum_ref[...], axis=0), axis=(0, 1), keepdims=True)
    exposure = EXPOSURE_KEY * jnp.exp(-total / pixels)
    for i in range(3):
        o_ref[0, i] = mapped_ref[i]
        scaled = exposure * second_ref[i]
        o_ref[1, i] = scaled / (1.0 + scaled)


def neighbours(low_source, high_source, axis):
    count = lax.axis_size(axis)
    forward = [(i, i + 1) for i in range(count - 1)]
    backward = [(target, source) for source, target in forward]
    return lax.ppermute(low_source, axis, forward), lax.ppermute(high_source, axis, backward)


def to_columns(part):
    part = lax.all_to_all(part.astype(jnp.float16), "depth", split_axis=0, concat_axis=0, tiled=True)
    return part.astype(f32)


def local(volume, tf_color, tf_opacity, light, background, exposure_prior):
    ylo, yhi = neighbours(volume[:, ROWS - 1], volume[:, 0], "tile")
    zlo, zhi = neighbours(volume[PLANES - 1], volume[0], "depth")
    front, back = march(volume, zlo, zhi, ylo, yhi, light, tf_color, tf_opacity)
    smem = pl.BlockSpec(memory_space=pltpu.SMEM)
    vmem = pl.BlockSpec(memory_space=pltpu.VMEM)
    image = jax.ShapeDtypeStruct((3, ROWS, WIDE), f32)
    front = to_columns(front)
    mapped, lum = pl.pallas_call(
        front_kernel,
        in_specs=[smem, smem, vmem],
        out_specs=[vmem] * 2,
        out_shape=[image, jax.ShapeDtypeStruct((8, LANES), f32)],
        name="front",
    )(background, exposure_prior, front)
    lum, back = lax.optimization_barrier((lum, back))
    sums = lax.all_gather(lum, ("tile", "depth"), axis=0, tiled=False)
    back = to_columns(back)
    second = pl.pallas_call(
        back_kernel, in_specs=[smem, vmem, vmem], out_specs=vmem, out_shape=image, name="back"
    )(background, front, back)
    pixels = ROWS * lax.axis_size("tile") * volume.shape[2]
    return pl.pallas_call(
        functools.partial(finish_kernel, float(pixels)),
        in_specs=[vmem] * 3,
        out_specs=vmem,
        out_shape=jax.ShapeDtypeStruct((2, 3, ROWS, WIDE), f32),
        name="finish",
    )(sums, mapped, second)


def solution(mesh):
    placed = (P("depth", "tile", None), P(), P(), P(), P(), P())
    return jax.shard_map(
        local, mesh=mesh, in_specs=placed, out_specs=P(None, None, "tile", "depth"), check_vma=False
    )
```

```python
import functools
import math

import jax
import jax.numpy as jnp
import numpy as np
from jax import lax
from jax.experimental import pallas as pl
from jax.experimental.pallas import tpu as pltpu
from jax.sharding import PartitionSpec as P

f32 = jnp.float32
bf16 = jnp.bfloat16
f16 = jnp.float16

BINS = 64
AMBIENT = 0.3
LUMA_EPS = 0.01
LOG_LOW = math.log(0.01)
LOG_HIGH = 0.05
EXPOSURE_KEY = 0.25
BIN_WIDTH = (LOG_HIGH - LOG_LOW) / (BINS - 1)

PLANES = 64
ROWS = 16
LANES = 128
DEPTH = 16
WIDE = 256
KNOTS = 16
VMEM = 58 * 1024 * 1024


def difference_matrices():
    base = np.zeros((512, WIDE), np.float32)
    for i in range(WIDE):
        base[LANES + i - 1, i] = -1
        base[LANES + i + 1, i] = 1
    first = base.copy()
    first[:LANES] = 0
    last = base.copy()
    last[LANES + WIDE :] = 0
    sy = np.zeros((2, 128, WIDE), np.float32)
    for e in range(2):
        for p in range(8):
            for r in range(ROWS):
                o = ROWS * p + r
                sy[e, o, o - 1 if r > 0 else 128 + 8 * e + p] = -1
                sy[e, o, o + 1 if r < ROWS - 1 else 144 + 8 * e + p] = 1
    return jnp.asarray(np.stack([first, base, last]), bf16), jnp.asarray(sy, bf16)


def pick(table, index):
    return jnp.take_along_axis(table, index, axis=0, mode="promise_in_bounds")


def halves(x):
    x = x.astype(f32)
    return [x[0:8], x[8:16]]


def march_kernel(
    light_ref, color_ref, opacity_ref, sxf_ref, sx_ref, sxl_ref, sy_ref,
    before_ref, cur_ref, next_ref, after_ref,
    zlo_ref, zhi_ref, ylo_ref, yhi_ref, ylon_ref, yhin_ref,
    front_ref, back_ref, dxa, dya, dxb, dyb, acc, table,
):
    s = pl.program_id(0)
    squares = light_ref[0] * light_ref[0] + light_ref[1] * light_ref[1] + light_ref[2] * light_ref[2]
    scale = (0.5 * (1.0 - AMBIENT)) * lax.rsqrt(jnp.full((8, LANES), squares + 1.0, f32))
    lz, ly, lx = light_ref[0] * scale, light_ref[1] * scale, light_ref[2] * scale

    def differences(g, part, pieces, matrix, before, after, block, dx, dy):
        ref, cols = block
        planes = pl.ds(pl.multiple_of(16 * g, 16), 16)
        if part == 0:
            wide = jnp.concatenate(
                [r[planes, :, c].reshape(256, c.stop - c.start) for r, c in pieces], axis=1
            )
            rows = pl.ds(pl.multiple_of(256 * g, 256), 256)
            dx[rows, :] = jnp.dot(wide, matrix[...], preferred_element_type=f32)
        else:
            edges = [r[planes, c] for r, c in (before, after)]
            fill = jnp.zeros((96, WIDE), bf16)
            for e in range(2):
                some = pl.ds(pl.multiple_of(16 * g + 8 * e, 8), 8)
                rows = pl.ds(pl.multiple_of(256 * g + 128 * e, 128), 128)
                tall = jnp.concatenate([ref[some, :, cols].reshape(128, WIDE), *edges, fill], axis=0)
                dy[rows, :] = jnp.dot(sy_ref[e], tall, preferred_element_type=f32)

    low, high = slice(0, WIDE), slice(WIDE, 2 * WIDE)
    first = (
        [(before_ref, slice(0, 128)), (cur_ref, slice(0, 384))],
        sxf_ref, (ylo_ref, low), (yhi_ref, low), (cur_ref, low), dxa, dya,
    )
    odd = (
        [(cur_ref, slice(128, 512)), (next_ref, slice(0, 128))],
        sxl_ref, (ylo_ref, high), (yhi_ref, high), (cur_ref, high), dxb, dyb,
    )
    even = (
        [(cur_ref, slice(384, 512)), (next_ref, low), (after_ref, slice(0, 128))],
        sx_ref, (ylon_ref, low), (yhin_ref, low), (next_ref, low), dxa, dya,
    )

    @pl.when(s == 0)
    def _():
        for k in range(4):
            f = [color_ref[k - 1, i] if k else opacity_ref[i] for i in range(KNOTS)]
            for j in range(8):
                mid = f[2 * j + 1]
                rise = f[2 * j + 2] - mid if j < 7 else 0.0
                for row, value in ((k, mid), (4 + k, mid - f[2 * j]), (8 + k, rise)):
                    table[8 * row + j : 8 * row + j + 1, :] = jnp.full((1, LANES), value, f32)
        for j in range(8):
            table[96 + j : 97 + j, :] = jnp.full((1, LANES), 2.0 * j + 1.0, f32)
        for g in range(4):
            for part in range(2):
                differences(g, part, *first)

    tb = [table[8 * k : 8 * k + 8, :] for k in range(13)]

    def sample(below, v, above, dx, dy, state):
        dz = above - below
        q = (dz * dz + 0.16) + (dy * dy + dx * dx)
        dot = (dz * lz + dy * ly) + dx * lx
        shade = (AMBIENT + 0.5 * (1.0 - AMBIENT)) + dot * lax.rsqrt(q)
        j = (v * 7.5).astype(jnp.int32)
        u = v * 15.0 - pick(tb[12], j)
        left = u < 0.0
        alpha, red, green, blue = [
            pick(tb[k], j) + jnp.where(left, pick(tb[4 + k], j), pick(tb[8 + k], j)) * u
            for k in range(4)
        ]
        w = alpha * shade
        keep = 1.0 - alpha
        p = [w * c for c in (red, green, blue)]
        through = state[3]
        return (
            [state[i] + through * p[i] for i in range(3)]
            + [through * keep]
            + [state[4 + i] * keep + p[i] for i in range(3)]
        )

    for half, (dx, dy, following) in enumerate(((dxa, dya, odd), (dxb, dyb, even))):
        for side in range(2):
            for h in range(2):
                for i in range(7):
                    acc[side, h, i] = jnp.full((8, LANES), 1.0 if i == 3 else 0.0, f32)

        def group(g, unused, half=half, dx=dx, dy=dy, following=following):
            for side in range(2):
                differences(g, side, *following)
                lanes = slice(LANES * side, LANES * side + LANES)
                at = WIDE * half + LANES * side
                cols = slice(at, at + LANES)
                lo = jnp.where(g == 0, zlo_ref[:, cols], cur_ref[jnp.maximum(16 * g - 1, 0), :, cols])
                hi = jnp.where(
                    g == 3, zhi_ref[:, cols], cur_ref[jnp.minimum(16 * g + 16, PLANES - 1), :, cols]
                )
                below, here = halves(lo), halves(cur_ref[16 * g, :, cols])
                state = [[acc[side, h, i] for i in range(7)] for h in range(2)]
                for p in range(16):
                    above = halves(cur_ref[16 * g + p + 1, :, cols] if p < 15 else hi)
                    for h in range(2):
                        rows = pl.ds(pl.multiple_of(256 * g + 16 * p + 8 * h, 8), 8)
                        state[h] = sample(
                            below[h], here[h], above[h], dx[rows, lanes], dy[rows, lanes], state[h]
                        )
                    below, here = here, above
                for h in range(2):
                    for i in range(7):
                        acc[side, h, i] = state[h][i]
            return unused

        lax.fori_loop(0, 4, group, 0, unroll=4)
        for side in range(2):
            lanes = slice(LANES * side, LANES * side + LANES)
            for h in range(2):
                rows = slice(8 * h, 8 * h + 8)
                for i in range(3):
                    front_ref[half, i, rows, lanes] = acc[side, h, i]
                    back_ref[half, i, rows, lanes] = acc[side, h, 4 + i]
                front_ref[half, 3, rows, lanes] = 1.0 - acc[side, h, 3]


def march(vol, zlo, zhi, ylo, yhi, light, tf_color, tf_opacity):
    sx, sy = difference_matrices()
    steps = DEPTH // 2

    def follower(s):
        return jnp.minimum(2 * s + 2, DEPTH - 1)

    def block(width, place):
        return pl.BlockSpec((PLANES, ROWS, width), lambda s: (0, 0, place(s)))

    def matrix(place):
        return pl.BlockSpec((None, 512, WIDE), lambda s: (place(s), 0, 0))

    def edge(rows, width, place):
        return pl.BlockSpec((rows, width), lambda s: (0, place(s)))

    smem = pl.BlockSpec(memory_space=pltpu.SMEM)
    return pl.pallas_call(
        march_kernel,
        grid=(steps,),
        in_specs=[
            smem,
            smem,
            smem,
            matrix(lambda s: 0),
            matrix(lambda s: 1),
            matrix(lambda s: jnp.where(s == steps - 1, 2, 1)),
            pl.BlockSpec((2, 128, WIDE), lambda s: (0, 0, 0)),
            block(LANES, lambda s: 0),
            block(2 * WIDE, lambda s: s),
            block(WIDE, follower),
            block(LANES, lambda s: jnp.minimum(4 * s + 6, 2 * DEPTH - 1)),
            edge(ROWS, 2 * WIDE, lambda s: s),
            edge(ROWS, 2 * WIDE, lambda s: s),
            edge(PLANES, 2 * WIDE, lambda s: s),
            edge(PLANES, 2 * WIDE, lambda s: s),
            edge(PLANES, WIDE, follower),
            edge(PLANES, WIDE, follower),
        ],
        out_specs=[
            pl.BlockSpec((2, n, ROWS, WIDE), lambda s: (s, 0, 0, 0)) for n in (4, 3)
        ],
        out_shape=[jax.ShapeDtypeStruct((DEPTH, n, ROWS, WIDE), f32) for n in (4, 3)],
        scratch_shapes=[pltpu.VMEM((PLANES * ROWS, WIDE), f32)] * 4
        + [pltpu.VMEM((2, 2, 7, 8, LANES), f32), pltpu.VMEM((104, LANES), f32)],
        compiler_params=pltpu.CompilerParams(vmem_limit_bytes=VMEM),
        cost_estimate=pl.CostEstimate(
            flops=400_000_000, bytes_accessed=24_000_000, transcendentals=4_000_000
        ),
        name="march",
    )(
        light, tf_color, tf_opacity, sx, sx, sx, sy, vol, vol, vol, vol,
        zlo, zhi, ylo, yhi, ylo, yhi,
    )


def front_kernel(bg_ref, prior_ref, s_ref, mapped_ref, lum_ref):
    total = jnp.zeros((8, LANES), f32)
    for c in range(2):
        cols = slice(LANES * c, LANES * c + LANES)
        front = [s_ref[0, i, :, cols] for i in range(3)]
        through = 1.0 - s_ref[0, 3, :, cols]
        for d in range(1, DEPTH):
            front = [front[i] + through * s_ref[d, i, :, cols] for i in range(3)]
            through = through - through * s_ref[d, 3, :, cols]
        front = [front[i] + through * bg_ref[i] for i in range(3)]
        lum = jnp.log(0.2126 * front[0] + 0.7152 * front[1] + 0.0722 * front[2] + LUMA_EPS)
        near = jnp.clip(lum, LOG_LOW, LOG_HIGH)
        term = near * jnp.maximum(0.0, 1.0 - jnp.abs(lum - near) * (1.0 / BIN_WIDTH))
        total = total + term[0:8] + term[8:16]
        for i in range(3):
            scaled = prior_ref[0] * front[i]
            mapped_ref[i, :, cols] = scaled / (1.0 + scaled)
    coarse = jnp.round(total * 64.0) * (1.0 / 64.0)
    lum_ref[...] = jnp.concatenate([coarse, total - coarse], axis=1)


def back_kernel(bg_ref, f_ref, s_ref, second_ref):
    for c in range(2):
        cols = slice(LANES * c, LANES * c + LANES)
        back = [s_ref[0, i, :, cols] for i in range(3)]
        through = 1.0 - f_ref[0, 3, :, cols]
        for d in range(1, DEPTH):
            keep = 1.0 - f_ref[d, 3, :, cols]
            back = [s_ref[d, i, :, cols] + keep * back[i] for i in range(3)]
            through = through * keep
        for i in range(3):
            second_ref[i, :, cols] = back[i] + through * bg_ref[i]


def finish_kernel(pixels, lum_ref, mapped_ref, second_ref, o_ref):
    total = jnp.sum(jnp.sum(lum_ref[...], axis=0), axis=(0, 1), keepdims=True)
    exposure = EXPOSURE_KEY * jnp.exp(-total / pixels)
    for i in range(3):
        o_ref[0, i] = mapped_ref[i]
        scaled = exposure * second_ref[i]
        o_ref[1, i] = scaled / (1.0 + scaled)


def neighbours(low_source, high_source, axis):
    count = lax.axis_size(axis)
    forward = [(i, i + 1) for i in range(count - 1)]
    backward = [(target, source) for source, target in forward]
    return lax.ppermute(low_source, axis, forward), lax.ppermute(high_source, axis, backward)


def exchange(part, axis):
    return lax.all_to_all(part, axis, split_axis=0, concat_axis=0, tiled=True)


def local(volume, tf_color, tf_opacity, light, background, exposure_prior):
    ylo, yhi = neighbours(volume[:, ROWS - 1], volume[:, 0], "tile")
    zlo, zhi = neighbours(volume[PLANES - 1], volume[0], "depth")
    front, back = march(volume, zlo, zhi, ylo, yhi, light, tf_color, tf_opacity)
    smem = pl.BlockSpec(memory_space=pltpu.SMEM)
    vmem = pl.BlockSpec(memory_space=pltpu.VMEM)
    image = jax.ShapeDtypeStruct((3, ROWS, WIDE), f32)
    front = exchange(front.astype(f16), "depth").astype(f32)
    mapped, lum = pl.pallas_call(
        front_kernel,
        in_specs=[smem, smem, vmem],
        out_specs=[vmem] * 2,
        out_shape=[image, jax.ShapeDtypeStruct((8, WIDE), f32)],
        name="front",
    )(background, exposure_prior, front)
    lum = jnp.broadcast_to(jnp.pad(lum, ((0, 8), (0, 0))), (DEPTH, 1, ROWS, WIDE))
    back = exchange(jnp.concatenate([back, lum], axis=1).astype(f16), "depth")
    sums = jnp.sum(back[:, 3, :8].astype(f32), axis=0)
    sums = sums[:, :LANES] + sums[:, LANES:]
    sums = exchange(jnp.broadcast_to(sums, (lax.axis_size("tile"), 8, LANES)), "tile")
    second = pl.pallas_call(
        back_kernel, in_specs=[smem, vmem, vmem], out_specs=vmem, out_shape=image, name="back"
    )(background, front, back[:, :3].astype(f32))
    pixels = ROWS * lax.axis_size("tile") * volume.shape[2]
    return pl.pallas_call(
        functools.partial(finish_kernel, float(pixels)),
        in_specs=[vmem] * 3,
        out_specs=vmem,
        out_shape=jax.ShapeDtypeStruct((2, 3, ROWS, WIDE), f32),
        name="finish",
    )(sums, mapped, second)


def solution(mesh):
    placed = (P("depth", "tile", None), P(), P(), P(), P(), P())
    return jax.shard_map(
        local, mesh=mesh, in_specs=placed, out_specs=P(None, None, "tile", "depth"), check_vma=False
    )
```

```python
import functools
import math

import jax
import jax.numpy as jnp
import numpy as np
from jax import lax
from jax.experimental import pallas as pl
from jax.experimental.pallas import tpu as pltpu
from jax.sharding import PartitionSpec as P

f32 = jnp.float32
bf16 = jnp.bfloat16
f16 = jnp.float16

BINS = 64
AMBIENT = 0.3
LUMA_EPS = 0.01
LOG_LOW = math.log(0.01)
LOG_HIGH = 0.05
EXPOSURE_KEY = 0.25
BIN_WIDTH = (LOG_HIGH - LOG_LOW) / (BINS - 1)

PLANES = 64
ROWS = 16
LANES = 128
DEPTH = 16
WIDE = 256
KNOTS = 16
VMEM = 50 * 1024 * 1024
SMALL = 16 * 1024 * 1024


def difference_matrices():
    base = np.zeros((512, WIDE), np.float32)
    for i in range(WIDE):
        base[LANES + i - 1, i] = -1
        base[LANES + i + 1, i] = 1
    first = base.copy()
    first[:LANES] = 0
    last = base.copy()
    last[LANES + WIDE :] = 0
    sy = np.zeros((2, 128, WIDE), np.float32)
    for e in range(2):
        for p in range(8):
            for r in range(ROWS):
                o = ROWS * p + r
                sy[e, o, o - 1 if r > 0 else 128 + 8 * e + p] = -1
                sy[e, o, o + 1 if r < ROWS - 1 else 144 + 8 * e + p] = 1
    return jnp.asarray(np.stack([first, base, last]), bf16), jnp.asarray(sy, bf16)


COLUMNWISE = lax.GatherDimensionNumbers(
    offset_dims=(),
    collapsed_slice_dims=(0,),
    start_index_map=(0,),
    operand_batching_dims=(1,),
    start_indices_batching_dims=(1,),
)


def pick(table, index):
    return lax.gather(
        table, index[:, :, None], COLUMNWISE, (1, 1), mode=lax.GatherScatterMode.PROMISE_IN_BOUNDS
    )


def halves(x):
    x = x.astype(f32)
    return [x[0:8], x[8:16]]


def march_kernel(
    light_ref, color_ref, opacity_ref, sxf_ref, sx_ref, sxl_ref, sy_ref,
    before_ref, cur_ref, next_ref, after_ref,
    zlo_ref, zhi_ref, ylo_ref, yhi_ref, ylon_ref, yhin_ref,
    front_ref, back_ref, dxa, dya, dxb, dyb, acc, table,
):
    s = pl.program_id(0)
    squares = light_ref[0] * light_ref[0] + light_ref[1] * light_ref[1] + light_ref[2] * light_ref[2]
    scale = (0.5 * (1.0 - AMBIENT)) * lax.rsqrt(jnp.full((8, LANES), squares + 1.0, f32))
    lz, ly, lx = light_ref[0] * scale, light_ref[1] * scale, light_ref[2] * scale

    def differences(g, part, pieces, matrix, before, after, block, dx, dy):
        ref, cols = block
        planes = pl.ds(pl.multiple_of(16 * g, 16), 16)
        if part == 0:
            wide = jnp.concatenate(
                [r[planes, :, c].reshape(256, c.stop - c.start) for r, c in pieces], axis=1
            )
            rows = pl.ds(pl.multiple_of(256 * g, 256), 256)
            dx[rows, :] = jnp.dot(wide, matrix[...], preferred_element_type=f32)
        else:
            edges = [r[planes, c] for r, c in (before, after)]
            fill = jnp.zeros((96, WIDE), bf16)
            for e in range(2):
                some = pl.ds(pl.multiple_of(16 * g + 8 * e, 8), 8)
                rows = pl.ds(pl.multiple_of(256 * g + 128 * e, 128), 128)
                tall = jnp.concatenate([ref[some, :, cols].reshape(128, WIDE), *edges, fill], axis=0)
                dy[rows, :] = jnp.dot(sy_ref[e], tall, preferred_element_type=f32)

    low, high = slice(0, WIDE), slice(WIDE, 2 * WIDE)
    first = (
        [(before_ref, slice(0, 128)), (cur_ref, slice(0, 384))],
        sxf_ref, (ylo_ref, low), (yhi_ref, low), (cur_ref, low), dxa, dya,
    )
    odd = (
        [(cur_ref, slice(128, 512)), (next_ref, slice(0, 128))],
        sxl_ref, (ylo_ref, high), (yhi_ref, high), (cur_ref, high), dxb, dyb,
    )
    even = (
        [(cur_ref, slice(384, 512)), (next_ref, low), (after_ref, slice(0, 128))],
        sx_ref, (ylon_ref, low), (yhin_ref, low), (next_ref, low), dxa, dya,
    )

    @pl.when(s == 0)
    def _():
        for k in range(4):
            f = [color_ref[k - 1, i] if k else opacity_ref[i] for i in range(KNOTS)]
            for j in range(8):
                mid = f[2 * j + 1]
                rise = f[2 * j + 2] - mid if j < 7 else 0.0
                for row, value in ((k, mid), (4 + k, 2.0 * (mid - f[2 * j])), (8 + k, 2.0 * rise)):
                    table[8 * row + j : 8 * row + j + 1, :] = jnp.full((1, LANES), value, f32)
        for j in range(8):
            table[96 + j : 97 + j, :] = jnp.full((1, LANES), j + 0.5, f32)
        for g in range(4):
            for part in range(2):
                differences(g, part, *first)

    tb = [table[8 * k : 8 * k + 8, :] for k in range(13)]

    def sample(below, v, above, dx, dy, state):
        v = v * 7.5
        dz = above - below
        q = (dz * dz + 0.16) + (dy * dy + dx * dx)
        dot = (dz * lz + dy * ly) + dx * lx
        shade = (AMBIENT + 0.5 * (1.0 - AMBIENT)) + dot * lax.rsqrt(q)
        j = v.astype(jnp.int32)
        u = v - pick(tb[12], j)
        left = u < 0.0
        alpha, red, green, blue = [
            pick(tb[k], j) + jnp.where(left, pick(tb[4 + k], j), pick(tb[8 + k], j)) * u
            for k in range(4)
        ]
        w = alpha * shade
        keep = 1.0 - alpha
        p = [w * c for c in (red, green, blue)]
        through = state[3]
        return (
            [state[i] + through * p[i] for i in range(3)]
            + [through * keep]
            + [state[4 + i] * keep + p[i] for i in range(3)]
        )

    for half, (dx, dy, following) in enumerate(((dxa, dya, odd), (dxb, dyb, even))):
        for side in range(2):
            for h in range(2):
                for i in range(7):
                    acc[side, h, i] = jnp.full((8, LANES), 1.0 if i == 3 else 0.0, f32)

        def group(g, unused, half=half, dx=dx, dy=dy, following=following):
            for side in range(2):
                differences(g, side, *following)
                lanes = slice(LANES * side, LANES * side + LANES)
                at = WIDE * half + LANES * side
                cols = slice(at, at + LANES)
                lo = jnp.where(g == 0, zlo_ref[:, cols], cur_ref[jnp.maximum(16 * g - 1, 0), :, cols])
                hi = jnp.where(
                    g == 3, zhi_ref[:, cols], cur_ref[jnp.minimum(16 * g + 16, PLANES - 1), :, cols]
                )
                below, here = halves(lo), halves(cur_ref[16 * g, :, cols])
                state = [[acc[side, h, i] for i in range(7)] for h in range(2)]
                for p in range(16):
                    above = halves(cur_ref[16 * g + p + 1, :, cols] if p < 15 else hi)
                    for h in range(2):
                        rows = pl.ds(pl.multiple_of(256 * g + 16 * p + 8 * h, 8), 8)
                        state[h] = sample(
                            below[h], here[h], above[h], dx[rows, lanes], dy[rows, lanes], state[h]
                        )
                    below, here = here, above
                for h in range(2):
                    for i in range(7):
                        acc[side, h, i] = state[h][i]
            return unused

        lax.fori_loop(0, 4, group, 0, unroll=4)
        for side in range(2):
            lanes = slice(LANES * side, LANES * side + LANES)
            for h in range(2):
                rows = slice(8 * h, 8 * h + 8)
                for i in range(3):
                    front_ref[half, i, rows, lanes] = acc[side, h, i]
                    back_ref[half, i, rows, lanes] = acc[side, h, 4 + i]
                front_ref[half, 3, rows, lanes] = 1.0 - acc[side, h, 3]


def march(vol, zlo, zhi, ylo, yhi, light, tf_color, tf_opacity):
    sx, sy = difference_matrices()
    steps = DEPTH // 2

    def follower(s):
        return jnp.minimum(2 * s + 2, DEPTH - 1)

    def block(width, place):
        return pl.BlockSpec((PLANES, ROWS, width), lambda s: (0, 0, place(s)))

    def matrix(place):
        return pl.BlockSpec((None, 512, WIDE), lambda s: (place(s), 0, 0))

    def edge(rows, width, place):
        return pl.BlockSpec((rows, width), lambda s: (0, place(s)))

    smem = pl.BlockSpec(memory_space=pltpu.SMEM)
    return pl.pallas_call(
        march_kernel,
        grid=(steps,),
        in_specs=[
            smem,
            smem,
            smem,
            matrix(lambda s: 0),
            matrix(lambda s: 1),
            matrix(lambda s: jnp.where(s == steps - 1, 2, 1)),
            pl.BlockSpec((2, 128, WIDE), lambda s: (0, 0, 0)),
            block(LANES, lambda s: 0),
            block(2 * WIDE, lambda s: s),
            block(WIDE, follower),
            block(LANES, lambda s: jnp.minimum(4 * s + 6, 2 * DEPTH - 1)),
            edge(ROWS, 2 * WIDE, lambda s: s),
            edge(ROWS, 2 * WIDE, lambda s: s),
            edge(PLANES, 2 * WIDE, lambda s: s),
            edge(PLANES, 2 * WIDE, lambda s: s),
            edge(PLANES, WIDE, follower),
            edge(PLANES, WIDE, follower),
        ],
        out_specs=[
            pl.BlockSpec((2, n, ROWS, WIDE), lambda s: (s, 0, 0, 0)) for n in (4, 3)
        ],
        out_shape=[jax.ShapeDtypeStruct((DEPTH, n, ROWS, WIDE), f32) for n in (4, 3)],
        scratch_shapes=[pltpu.VMEM((PLANES * ROWS, WIDE), f32)] * 4
        + [pltpu.VMEM((2, 2, 7, 8, LANES), f32), pltpu.VMEM((104, LANES), f32)],
        compiler_params=pltpu.CompilerParams(vmem_limit_bytes=VMEM),
        cost_estimate=pl.CostEstimate(
            flops=400_000_000, bytes_accessed=24_000_000, transcendentals=4_000_000
        ),
        name="march",
    )(
        light, tf_color, tf_opacity, sx, sx, sx, sy, vol, vol, vol, vol,
        zlo, zhi, ylo, yhi, ylo, yhi,
    )


def edges_kernel(pick_ref, v_ref, zlast_ref, zfirst_ref, ylast_ref, yfirst_ref):
    zlast_ref[...] = v_ref[PLANES - 1]
    zfirst_ref[...] = v_ref[0]
    width = v_ref.shape[2]
    for g in range(4):
        planes = slice(16 * g, 16 * g + 16)
        rows = v_ref[planes].reshape(256, width)
        rows = jnp.dot(pick_ref[...], rows, preferred_element_type=f32).astype(bf16)
        ylast_ref[planes, :] = rows[:16]
        yfirst_ref[planes, :] = rows[16:]


def edges(vol):
    width = 2048
    choose = np.zeros((32, 256), np.float32)
    for p in range(16):
        choose[p, ROWS * p + ROWS - 1] = 1
        choose[16 + p, ROWS * p] = 1
    return pl.pallas_call(
        edges_kernel,
        grid=(vol.shape[2] // width,),
        in_specs=[
            pl.BlockSpec((32, 256), lambda s: (0, 0)),
            pl.BlockSpec((PLANES, ROWS, width), lambda s: (0, 0, s)),
        ],
        out_specs=[pl.BlockSpec((n, width), lambda s: (0, s)) for n in (ROWS, ROWS, PLANES, PLANES)],
        out_shape=[
            jax.ShapeDtypeStruct((n, vol.shape[2]), bf16) for n in (ROWS, ROWS, PLANES, PLANES)
        ],
        compiler_params=pltpu.CompilerParams(vmem_limit_bytes=58 * 1024 * 1024),
        name="edges",
    )(jnp.asarray(choose, bf16), vol)


def front_kernel(bg_ref, prior_ref, s_ref, mapped_ref, lum_ref):
    total = jnp.zeros((8, LANES), f32)
    for c in range(2):
        cols = slice(LANES * c, LANES * c + LANES)
        front = [s_ref[0, i, :, cols] for i in range(3)]
        through = 1.0 - s_ref[0, 3, :, cols]
        for d in range(1, DEPTH):
            front = [front[i] + through * s_ref[d, i, :, cols] for i in range(3)]
            through = through - through * s_ref[d, 3, :, cols]
        front = [front[i] + through * bg_ref[i] for i in range(3)]
        lum = jnp.log(0.2126 * front[0] + 0.7152 * front[1] + 0.0722 * front[2] + LUMA_EPS)
        near = jnp.clip(lum, LOG_LOW, LOG_HIGH)
        term = near * jnp.maximum(0.0, 1.0 - jnp.abs(lum - near) * (1.0 / BIN_WIDTH))
        total = total + term[0:8] + term[8:16]
        for i in range(3):
            scaled = prior_ref[0] * front[i]
            mapped_ref[i, :, cols] = scaled / (1.0 + scaled)
    coarse = jnp.round(total * 64.0) * (1.0 / 64.0)
    lum_ref[...] = jnp.concatenate([coarse, total - coarse], axis=1)


def back_kernel(bg_ref, f_ref, s_ref, second_ref):
    for c in range(2):
        cols = slice(LANES * c, LANES * c + LANES)
        back = [s_ref[0, i, :, cols] for i in range(3)]
        through = 1.0 - f_ref[0, 3, :, cols]
        for d in range(1, DEPTH):
            keep = 1.0 - f_ref[d, 3, :, cols]
            back = [s_ref[d, i, :, cols] + keep * back[i] for i in range(3)]
            through = through * keep
        for i in range(3):
            second_ref[i, :, cols] = back[i] + through * bg_ref[i]


def finish_kernel(pixels, lum_ref, mapped_ref, second_ref, o_ref):
    total = jnp.sum(jnp.sum(lum_ref[...], axis=0), axis=(0, 1), keepdims=True)
    exposure = EXPOSURE_KEY * jnp.exp(-total / pixels)
    for i in range(3):
        o_ref[0, i] = mapped_ref[i]
        scaled = exposure * second_ref[i]
        o_ref[1, i] = scaled / (1.0 + scaled)


def neighbours(low_source, high_source, axis):
    count = lax.axis_size(axis)
    forward = [(i, i + 1) for i in range(count - 1)]
    backward = [(target, source) for source, target in forward]
    return lax.ppermute(low_source, axis, forward), lax.ppermute(high_source, axis, backward)


def exchange(part, axis):
    return lax.all_to_all(part, axis, split_axis=0, concat_axis=0, tiled=True)


def local(volume, tf_color, tf_opacity, light, background, exposure_prior):
    zlast, zfirst, ylast, yfirst = edges(volume)
    ylo, yhi = neighbours(ylast, yfirst, "tile")
    zlo, zhi = neighbours(zlast, zfirst, "depth")
    front, back = march(volume, zlo, zhi, ylo, yhi, light, tf_color, tf_opacity)
    smem = pl.BlockSpec(memory_space=pltpu.SMEM)
    vmem = pl.BlockSpec(memory_space=pltpu.VMEM)
    image = jax.ShapeDtypeStruct((3, ROWS, WIDE), f32)
    front = exchange(front.astype(f16), "depth").astype(f32)
    mapped, lum = pl.pallas_call(
        front_kernel,
        in_specs=[smem, smem, vmem],
        out_specs=[vmem] * 2,
        out_shape=[image, jax.ShapeDtypeStruct((8, WIDE), f32)],
        compiler_params=pltpu.CompilerParams(vmem_limit_bytes=SMALL),
        name="front",
    )(background, exposure_prior, front)
    lum = jnp.broadcast_to(jnp.pad(lum, ((0, 8), (0, 0))), (DEPTH, 1, ROWS, WIDE))
    back = exchange(jnp.concatenate([back, lum], axis=1).astype(f16), "depth")
    sums = jnp.sum(back[:, 3, :8].astype(f32), axis=0)
    sums = sums[:, :LANES] + sums[:, LANES:]
    sums = exchange(jnp.broadcast_to(sums, (lax.axis_size("tile"), 8, LANES)), "tile")
    second = pl.pallas_call(
        back_kernel,
        in_specs=[smem, vmem, vmem],
        out_specs=vmem,
        out_shape=image,
        compiler_params=pltpu.CompilerParams(vmem_limit_bytes=SMALL),
        name="back",
    )(background, front, back[:, :3].astype(f32))
    pixels = ROWS * lax.axis_size("tile") * volume.shape[2]
    return pl.pallas_call(
        functools.partial(finish_kernel, float(pixels)),
        in_specs=[vmem] * 3,
        out_specs=vmem,
        out_shape=jax.ShapeDtypeStruct((2, 3, ROWS, WIDE), f32),
        compiler_params=pltpu.CompilerParams(vmem_limit_bytes=SMALL),
        name="finish",
    )(sums, mapped, second)


def solution(mesh):
    placed = (P("depth", "tile", None), P(), P(), P(), P(), P())
    return jax.shard_map(
        local, mesh=mesh, in_specs=placed, out_specs=P(None, None, "tile", "depth"), check_vma=False
    )
```

```python
import functools
import math

import jax
import jax.numpy as jnp
import numpy as np
from jax import lax
from jax.experimental import pallas as pl
from jax.experimental.pallas import tpu as pltpu
from jax.sharding import PartitionSpec as P

f32 = jnp.float32
bf16 = jnp.bfloat16
f16 = jnp.float16

BINS = 64
AMBIENT = 0.3
LUMA_EPS = 0.01
LOG_LOW = math.log(0.01)
LOG_HIGH = 0.05
EXPOSURE_KEY = 0.25
BIN_WIDTH = (LOG_HIGH - LOG_LOW) / (BINS - 1)

PLANES = 64
ROWS = 16
LANES = 128
DEPTH = 16
WIDE = 256
KNOTS = 16
VMEM = 50 * 1024 * 1024
SMALL = 16 * 1024 * 1024


def difference_matrices():
    base = np.zeros((512, WIDE), np.float32)
    for i in range(WIDE):
        base[LANES + i - 1, i] = -1
        base[LANES + i + 1, i] = 1
    first = base.copy()
    first[:LANES] = 0
    last = base.copy()
    last[LANES + WIDE :] = 0
    sy = np.zeros((2, 2, 128, WIDE), np.float32)
    for e in range(2):
        for p in range(8):
            for r in range(ROWS):
                o = ROWS * p + r
                for odd in range(2):
                    before = 144 - 16 * odd + 8 * e + p
                    after = 128 + 16 * odd + 8 * e + p
                    sy[odd, e, o, o - 1 if r > 0 else before] = -1
                    sy[odd, e, o, o + 1 if r < ROWS - 1 else after] = 1
    return jnp.asarray(np.stack([first, base, last]), bf16), jnp.asarray(sy, bf16)


COLUMNWISE = lax.GatherDimensionNumbers(
    offset_dims=(),
    collapsed_slice_dims=(0,),
    start_index_map=(0,),
    operand_batching_dims=(1,),
    start_indices_batching_dims=(1,),
)


def pick(table, index):
    return lax.gather(
        table, index[:, :, None], COLUMNWISE, (1, 1), mode=lax.GatherScatterMode.PROMISE_IN_BOUNDS
    )


def halves(x):
    x = x.astype(f32)
    return [x[0:8], x[8:16]]


def march_kernel(
    odd_ref, light_ref, color_ref, opacity_ref, sxf_ref, sx_ref, sxl_ref, sy_ref,
    before_ref, cur_ref, next_ref, after_ref,
    za_ref, zb_ref, ya_ref, yb_ref, yan_ref, ybn_ref,
    front_ref, back_ref, dxa, dya, dxb, dyb, acc, table,
):
    s = pl.program_id(0)
    squares = light_ref[0] * light_ref[0] + light_ref[1] * light_ref[1] + light_ref[2] * light_ref[2]
    scale = (0.5 * (1.0 - AMBIENT)) * lax.rsqrt(jnp.full((8, LANES), squares + 1.0, f32))
    lz, ly, lx = light_ref[0] * scale, light_ref[1] * scale, light_ref[2] * scale

    def differences(g, part, pieces, matrix, before, after, block, dx, dy):
        ref, cols = block
        planes = pl.ds(pl.multiple_of(16 * g, 16), 16)
        if part == 0:
            wide = jnp.concatenate(
                [r[planes, :, c].reshape(256, c.stop - c.start) for r, c in pieces], axis=1
            )
            rows = pl.ds(pl.multiple_of(256 * g, 256), 256)
            dx[rows, :] = jnp.dot(wide, matrix[...], preferred_element_type=f32)
        else:
            edges = [r[planes, c] for r, c in (before, after)]
            fill = jnp.zeros((96, WIDE), bf16)
            for e in range(2):
                some = pl.ds(pl.multiple_of(16 * g + 8 * e, 8), 8)
                rows = pl.ds(pl.multiple_of(256 * g + 128 * e, 128), 128)
                tall = jnp.concatenate([ref[some, :, cols].reshape(128, WIDE), *edges, fill], axis=0)
                dy[rows, :] = jnp.dot(sy_ref[odd_ref[0], e], tall, preferred_element_type=f32)

    low, high = slice(0, WIDE), slice(WIDE, 2 * WIDE)
    first = (
        [(before_ref, slice(0, 128)), (cur_ref, slice(0, 384))],
        sxf_ref, (ya_ref, low), (yb_ref, low), (cur_ref, low), dxa, dya,
    )
    odd = (
        [(cur_ref, slice(128, 512)), (next_ref, slice(0, 128))],
        sxl_ref, (ya_ref, high), (yb_ref, high), (cur_ref, high), dxb, dyb,
    )
    even = (
        [(cur_ref, slice(384, 512)), (next_ref, low), (after_ref, slice(0, 128))],
        sx_ref, (yan_ref, low), (ybn_ref, low), (next_ref, low), dxa, dya,
    )

    @pl.when(s == 0)
    def _():
        for k in range(4):
            f = [color_ref[k - 1, i] if k else opacity_ref[i] for i in range(KNOTS)]
            for j in range(8):
                mid = f[2 * j + 1]
                rise = f[2 * j + 2] - mid if j < 7 else 0.0
                for row, value in ((k, mid), (4 + k, 2.0 * (mid - f[2 * j])), (8 + k, 2.0 * rise)):
                    table[8 * row + j : 8 * row + j + 1, :] = jnp.full((1, LANES), value, f32)
        for j in range(8):
            table[96 + j : 97 + j, :] = jnp.full((1, LANES), j + 0.5, f32)
        for g in range(4):
            for part in range(2):
                differences(g, part, *first)

    tb = [table[8 * k : 8 * k + 8, :] for k in range(13)]

    def sample(below, v, above, dx, dy, state):
        v = v * 7.5
        dz = above - below
        q = (dz * dz + 0.16) + (dy * dy + dx * dx)
        dot = (dz * lz + dy * ly) + dx * lx
        shade = (AMBIENT + 0.5 * (1.0 - AMBIENT)) + dot * lax.rsqrt(q)
        j = v.astype(jnp.int32)
        u = v - pick(tb[12], j)
        left = u < 0.0
        alpha, red, green, blue = [
            pick(tb[k], j) + jnp.where(left, pick(tb[4 + k], j), pick(tb[8 + k], j)) * u
            for k in range(4)
        ]
        w = alpha * shade
        keep = 1.0 - alpha
        p = [w * c for c in (red, green, blue)]
        through = state[3]
        return (
            [state[i] + through * p[i] for i in range(3)]
            + [through * keep]
            + [state[4 + i] * keep + p[i] for i in range(3)]
        )

    for half, (dx, dy, following) in enumerate(((dxa, dya, odd), (dxb, dyb, even))):
        for side in range(2):
            for h in range(2):
                for i in range(7):
                    acc[side, h, i] = jnp.full((8, LANES), 1.0 if i == 3 else 0.0, f32)

        for g in range(4):
            for side in range(2):
                differences(g, side, *following)
                lanes = slice(LANES * side, LANES * side + LANES)
                at = WIDE * half + LANES * side
                cols = slice(at, at + LANES)
                ends = [za_ref[:, cols].astype(f32), zb_ref[:, cols].astype(f32)]
                swap = odd_ref[1] == 1
                lo = jnp.where(swap, *ends) if g == 0 else cur_ref[16 * g - 1, :, cols]
                hi = jnp.where(swap, *ends[::-1]) if g == 3 else cur_ref[16 * g + 16, :, cols]
                below, here = halves(lo), halves(cur_ref[16 * g, :, cols])
                state = [[acc[side, h, i] for i in range(7)] for h in range(2)]
                for p in range(16):
                    above = halves(cur_ref[16 * g + p + 1, :, cols] if p < 15 else hi)
                    for h in range(2):
                        rows = pl.ds(pl.multiple_of(256 * g + 16 * p + 8 * h, 8), 8)
                        state[h] = sample(
                            below[h], here[h], above[h], dx[rows, lanes], dy[rows, lanes], state[h]
                        )
                    below, here = here, above
                for h in range(2):
                    for i in range(7):
                        acc[side, h, i] = state[h][i]

        for side in range(2):
            lanes = slice(LANES * side, LANES * side + LANES)
            for h in range(2):
                rows = slice(8 * h, 8 * h + 8)
                for i in range(3):
                    front_ref[half, i, rows, lanes] = acc[side, h, i]
                    back_ref[half, i, rows, lanes] = acc[side, h, 4 + i]
                front_ref[half, 3, rows, lanes] = 1.0 - acc[side, h, 3]


def march(vol, odd, za, zb, ya, yb, light, tf_color, tf_opacity):
    sx, sy = difference_matrices()
    steps = DEPTH // 2

    def follower(s):
        return jnp.minimum(2 * s + 2, DEPTH - 1)

    def block(width, place):
        return pl.BlockSpec((PLANES, ROWS, width), lambda s: (0, 0, place(s)))

    def matrix(place):
        return pl.BlockSpec((None, 512, WIDE), lambda s: (place(s), 0, 0))

    def edge(rows, width, place):
        return pl.BlockSpec((rows, width), lambda s: (0, place(s)))

    smem = pl.BlockSpec(memory_space=pltpu.SMEM)
    return pl.pallas_call(
        march_kernel,
        grid=(steps,),
        in_specs=[
            smem,
            smem,
            smem,
            smem,
            matrix(lambda s: 0),
            matrix(lambda s: 1),
            matrix(lambda s: jnp.where(s == steps - 1, 2, 1)),
            pl.BlockSpec((2, 2, 128, WIDE), lambda s: (0, 0, 0, 0)),
            block(LANES, lambda s: 0),
            block(2 * WIDE, lambda s: s),
            block(WIDE, follower),
            block(LANES, lambda s: jnp.minimum(4 * s + 6, 2 * DEPTH - 1)),
            edge(ROWS, 2 * WIDE, lambda s: s),
            edge(ROWS, 2 * WIDE, lambda s: s),
            edge(PLANES, 2 * WIDE, lambda s: s),
            edge(PLANES, 2 * WIDE, lambda s: s),
            edge(PLANES, WIDE, follower),
            edge(PLANES, WIDE, follower),
        ],
        out_specs=[
            pl.BlockSpec((2, n, ROWS, WIDE), lambda s: (s, 0, 0, 0)) for n in (4, 3)
        ],
        out_shape=[jax.ShapeDtypeStruct((DEPTH, n, ROWS, WIDE), f32) for n in (4, 3)],
        scratch_shapes=[pltpu.VMEM((PLANES * ROWS, WIDE), f32)] * 4
        + [pltpu.VMEM((2, 2, 7, 8, LANES), f32), pltpu.VMEM((104, LANES), f32)],
        compiler_params=pltpu.CompilerParams(vmem_limit_bytes=VMEM),
        cost_estimate=pl.CostEstimate(
            flops=400_000_000, bytes_accessed=24_000_000, transcendentals=4_000_000
        ),
        name="march",
    )(
        odd, light, tf_color, tf_opacity, sx, sx, sx, sy, vol, vol, vol, vol,
        za, zb, ya, yb, ya, yb,
    )


def edges_kernel(odd_ref, pick_ref, v_ref, za_ref, zb_ref, ya_ref, yb_ref):
    za_ref[...] = v_ref[(PLANES - 1) * (1 - odd_ref[1])]
    zb_ref[...] = v_ref[(PLANES - 1) * odd_ref[1]]
    width = v_ref.shape[2]
    for g in range(4):
        planes = slice(16 * g, 16 * g + 16)
        rows = v_ref[planes].reshape(256, width)
        rows = jnp.dot(pick_ref[odd_ref[0]], rows, preferred_element_type=f32).astype(bf16)
        ya_ref[planes, :] = rows[:16]
        yb_ref[planes, :] = rows[16:]


def edges(vol, odd):
    width = 2048
    choose = np.zeros((2, 32, 256), np.float32)
    for p in range(16):
        for o in range(2):
            choose[o, 16 * o + p, ROWS * p + ROWS - 1] = 1
            choose[o, 16 - 16 * o + p, ROWS * p] = 1
    return pl.pallas_call(
        edges_kernel,
        grid=(vol.shape[2] // width,),
        in_specs=[
            pl.BlockSpec(memory_space=pltpu.SMEM),
            pl.BlockSpec((2, 32, 256), lambda s: (0, 0, 0)),
            pl.BlockSpec((PLANES, ROWS, width), lambda s: (0, 0, s)),
        ],
        out_specs=[pl.BlockSpec((n, width), lambda s: (0, s)) for n in (ROWS, ROWS, PLANES, PLANES)],
        out_shape=[
            jax.ShapeDtypeStruct((n, vol.shape[2]), bf16) for n in (ROWS, ROWS, PLANES, PLANES)
        ],
        compiler_params=pltpu.CompilerParams(vmem_limit_bytes=58 * 1024 * 1024),
        name="edges",
    )(odd, jnp.asarray(choose, bf16), vol)


def front_kernel(bg_ref, prior_ref, s_ref, mapped_ref, lum_ref):
    total = jnp.zeros((8, LANES), f32)
    for c in range(2):
        cols = slice(LANES * c, LANES * c + LANES)
        front = [s_ref[0, i, :, cols] for i in range(3)]
        through = 1.0 - s_ref[0, 3, :, cols]
        for d in range(1, DEPTH):
            front = [front[i] + through * s_ref[d, i, :, cols] for i in range(3)]
            through = through - through * s_ref[d, 3, :, cols]
        front = [front[i] + through * bg_ref[i] for i in range(3)]
        lum = jnp.log(0.2126 * front[0] + 0.7152 * front[1] + 0.0722 * front[2] + LUMA_EPS)
        near = jnp.clip(lum, LOG_LOW, LOG_HIGH)
        term = near * jnp.maximum(0.0, 1.0 - jnp.abs(lum - near) * (1.0 / BIN_WIDTH))
        total = total + term[0:8] + term[8:16]
        for i in range(3):
            scaled = prior_ref[0] * front[i]
            mapped_ref[i, :, cols] = scaled / (1.0 + scaled)
    coarse = jnp.round(total * 64.0) * (1.0 / 64.0)
    lum_ref[...] = jnp.concatenate([coarse, total - coarse], axis=1)


def back_kernel(bg_ref, f_ref, s_ref, second_ref):
    for c in range(2):
        cols = slice(LANES * c, LANES * c + LANES)
        back = [s_ref[0, i, :, cols] for i in range(3)]
        through = 1.0 - f_ref[0, 3, :, cols]
        for d in range(1, DEPTH):
            keep = 1.0 - f_ref[d, 3, :, cols]
            back = [s_ref[d, i, :, cols] + keep * back[i] for i in range(3)]
            through = through * keep
        for i in range(3):
            second_ref[i, :, cols] = back[i] + through * bg_ref[i]


def finish_kernel(pixels, lum_ref, mapped_ref, second_ref, o_ref):
    total = jnp.sum(jnp.sum(lum_ref[...], axis=0), axis=(0, 1), keepdims=True)
    exposure = EXPOSURE_KEY * jnp.exp(-total / pixels)
    for i in range(3):
        o_ref[0, i] = mapped_ref[i]
        scaled = exposure * second_ref[i]
        o_ref[1, i] = scaled / (1.0 + scaled)


def swap(first, second, axis):
    count = lax.axis_size(axis)
    pairs = [(i, i ^ 1) for i in range(count)]
    others = [(i, i + 1 if i % 2 else i - 1) for i in range(1, count - 1)]
    return lax.ppermute(first, axis, pairs), lax.ppermute(second, axis, others)


def exchange(part, axis):
    return lax.all_to_all(part, axis, split_axis=0, concat_axis=0, tiled=True)


def local(volume, tf_color, tf_opacity, light, background, exposure_prior):
    odd = jnp.stack([lax.axis_index(axis) % 2 for axis in ("tile", "depth")])
    za, zb, ya, yb = edges(volume, odd)
    ya, yb = swap(ya, yb, "tile")
    za, zb = swap(za, zb, "depth")
    front, back = march(volume, odd, za, zb, ya, yb, light, tf_color, tf_opacity)
    smem = pl.BlockSpec(memory_space=pltpu.SMEM)
    vmem = pl.BlockSpec(memory_space=pltpu.VMEM)
    image = jax.ShapeDtypeStruct((3, ROWS, WIDE), f32)
    front = exchange(front.astype(f16), "depth").astype(f32)
    mapped, lum = pl.pallas_call(
        front_kernel,
        in_specs=[smem, smem, vmem],
        out_specs=[vmem] * 2,
        out_shape=[image, jax.ShapeDtypeStruct((8, WIDE), f32)],
        compiler_params=pltpu.CompilerParams(vmem_limit_bytes=SMALL),
        name="front",
    )(background, exposure_prior, front)
    lum = jnp.broadcast_to(jnp.pad(lum, ((0, 8), (0, 0))), (DEPTH, 1, ROWS, WIDE))
    back = exchange(jnp.concatenate([back, lum], axis=1).astype(f16), "depth")
    sums = jnp.sum(back[:, 3, :8].astype(f32), axis=0)
    sums = sums[:, :LANES] + sums[:, LANES:]
    sums = exchange(jnp.broadcast_to(sums, (lax.axis_size("tile"), 8, LANES)), "tile")
    second = pl.pallas_call(
        back_kernel,
        in_specs=[smem, vmem, vmem],
        out_specs=vmem,
        out_shape=image,
        compiler_params=pltpu.CompilerParams(vmem_limit_bytes=SMALL),
        name="back",
    )(background, front, back[:, :3].astype(f32))
    pixels = ROWS * lax.axis_size("tile") * volume.shape[2]
    return pl.pallas_call(
        functools.partial(finish_kernel, float(pixels)),
        in_specs=[vmem] * 3,
        out_specs=vmem,
        out_shape=jax.ShapeDtypeStruct((2, 3, ROWS, WIDE), f32),
        compiler_params=pltpu.CompilerParams(vmem_limit_bytes=SMALL),
        name="finish",
    )(sums, mapped, second)


def solution(mesh):
    placed = (P("depth", "tile", None), P(), P(), P(), P(), P())
    return jax.shard_map(
        local, mesh=mesh, in_specs=placed, out_specs=P(None, None, "tile", "depth"), check_vma=False
    )
```

```python
import functools
import math

import jax
import jax.numpy as jnp
import numpy as np
from jax import lax
from jax.experimental import pallas as pl
from jax.experimental.pallas import tpu as pltpu
from jax.sharding import PartitionSpec as P

f32 = jnp.float32
bf16 = jnp.bfloat16
f16 = jnp.float16

BINS = 64
AMBIENT = 0.3
LUMA_EPS = 0.01
LOG_LOW = math.log(0.01)
LOG_HIGH = 0.05
EXPOSURE_KEY = 0.25
BIN_WIDTH = (LOG_HIGH - LOG_LOW) / (BINS - 1)

PLANES = 64
ROWS = 16
LANES = 128
DEPTH = 16
WIDE = 256
KNOTS = 16
VMEM = 44 * 1024 * 1024
SMALL = 16 * 1024 * 1024


def difference_matrices():
    base = np.zeros((512, WIDE), np.float32)
    for i in range(WIDE):
        base[LANES + i - 1, i] = -1
        base[LANES + i + 1, i] = 1
    first = base.copy()
    first[:LANES] = 0
    last = base.copy()
    last[LANES + WIDE :] = 0
    sy = np.zeros((2, 2, 128, WIDE), np.float32)
    for e in range(2):
        for p in range(8):
            for r in range(ROWS):
                o = ROWS * p + r
                for odd in range(2):
                    before = 144 - 16 * odd + 8 * e + p
                    after = 128 + 16 * odd + 8 * e + p
                    sy[odd, e, o, o - 1 if r > 0 else before] = -1
                    sy[odd, e, o, o + 1 if r < ROWS - 1 else after] = 1
    return jnp.asarray(np.stack([first, base, last]), bf16), jnp.asarray(sy, bf16)


COLUMNWISE = lax.GatherDimensionNumbers(
    offset_dims=(),
    collapsed_slice_dims=(0,),
    start_index_map=(0,),
    operand_batching_dims=(1,),
    start_indices_batching_dims=(1,),
)


def pick(table, index):
    return lax.gather(
        table, index[:, :, None], COLUMNWISE, (1, 1), mode=lax.GatherScatterMode.PROMISE_IN_BOUNDS
    )


def halves(x):
    x = x.astype(f32)
    return [x[0:8], x[8:16]]


def march_kernel(
    odd_ref, light_ref, color_ref, opacity_ref, sxf_ref, sx_ref, sxl_ref, sy_ref,
    before_ref, cur_ref, next_ref, after_ref,
    za_ref, zb_ref, ya_ref, yb_ref, yan_ref, ybn_ref,
    front_ref, back_ref, dxa, dya, dxb, dyb, acc, table,
):
    s = pl.program_id(0)
    squares = light_ref[0] * light_ref[0] + light_ref[1] * light_ref[1] + light_ref[2] * light_ref[2]
    scale = (0.5 * (1.0 - AMBIENT)) * lax.rsqrt(jnp.full((8, LANES), squares + 1.0, f32))
    lz, ly, lx = light_ref[0] * scale, light_ref[1] * scale, light_ref[2] * scale

    def differences(g, part, pieces, matrix, before, after, block, dx, dy):
        ref, cols = block
        planes = pl.ds(pl.multiple_of(16 * g, 16), 16)
        if part == 0:
            wide = jnp.concatenate(
                [r[planes, :, c].reshape(256, c.stop - c.start) for r, c in pieces], axis=1
            )
            rows = pl.ds(pl.multiple_of(256 * g, 256), 256)
            dx[rows, :] = jnp.dot(wide, matrix[...], preferred_element_type=f32)
        else:
            edges = [r[planes, c] for r, c in (before, after)]
            fill = jnp.zeros((96, WIDE), bf16)
            for e in range(2):
                some = pl.ds(pl.multiple_of(16 * g + 8 * e, 8), 8)
                rows = pl.ds(pl.multiple_of(256 * g + 128 * e, 128), 128)
                tall = jnp.concatenate([ref[some, :, cols].reshape(128, WIDE), *edges, fill], axis=0)
                dy[rows, :] = jnp.dot(sy_ref[odd_ref[0], e], tall, preferred_element_type=f32)

    low, high = slice(0, WIDE), slice(WIDE, 2 * WIDE)
    first = (
        [(before_ref, slice(0, 128)), (cur_ref, slice(0, 384))],
        sxf_ref, (ya_ref, low), (yb_ref, low), (cur_ref, low), dxa, dya,
    )
    odd = (
        [(cur_ref, slice(128, 512)), (next_ref, slice(0, 128))],
        sxl_ref, (ya_ref, high), (yb_ref, high), (cur_ref, high), dxb, dyb,
    )
    even = (
        [(cur_ref, slice(384, 512)), (next_ref, low), (after_ref, slice(0, 128))],
        sx_ref, (yan_ref, low), (ybn_ref, low), (next_ref, low), dxa, dya,
    )

    @pl.when(s == 0)
    def _():
        for k in range(4):
            f = [color_ref[k - 1, i] if k else opacity_ref[i] for i in range(KNOTS)]
            for j in range(8):
                mid = f[2 * j + 1]
                rise = f[2 * j + 2] - mid if j < 7 else 0.0
                for row, value in ((k, mid), (4 + k, 2.0 * (mid - f[2 * j])), (8 + k, 2.0 * rise)):
                    table[8 * row + j : 8 * row + j + 1, :] = jnp.full((1, LANES), value, f32)
        for j in range(8):
            table[96 + j : 97 + j, :] = jnp.full((1, LANES), j + 0.5, f32)
        for g in range(4):
            for part in range(2):
                differences(g, part, *first)

    tb = [table[8 * k : 8 * k + 8, :] for k in range(13)]

    def sample(below, v, above, dx, dy, state):
        v = v * 7.5
        dz = above - below
        q = (dz * dz + 0.16) + (dy * dy + dx * dx)
        dot = (dz * lz + dy * ly) + dx * lx
        shade = (AMBIENT + 0.5 * (1.0 - AMBIENT)) + dot * lax.rsqrt(q)
        j = v.astype(jnp.int32)
        u = v - pick(tb[12], j)
        left = u < 0.0
        alpha, red, green, blue = [
            pick(tb[k], j) + jnp.where(left, pick(tb[4 + k], j), pick(tb[8 + k], j)) * u
            for k in range(4)
        ]
        w = alpha * shade
        keep = 1.0 - alpha
        p = [w * c for c in (red, green, blue)]
        through = state[3]
        return (
            [state[i] + through * p[i] for i in range(3)]
            + [through * keep]
            + [state[4 + i] * keep + p[i] for i in range(3)]
        )

    for half, (dx, dy, following) in enumerate(((dxa, dya, odd), (dxb, dyb, even))):
        for side in range(2):
            for h in range(2):
                for i in range(7):
                    acc[side, h, i] = jnp.full((8, LANES), 1.0 if i == 3 else 0.0, f32)

        for g in range(4):
            for side in range(2):
                differences(g, side, *following)
                lanes = slice(LANES * side, LANES * side + LANES)
                at = WIDE * half + LANES * side
                cols = slice(at, at + LANES)
                ends = [za_ref[:, cols].astype(f32), zb_ref[:, cols].astype(f32)]
                swap = odd_ref[1] == 1
                lo = jnp.where(swap, *ends) if g == 0 else cur_ref[16 * g - 1, :, cols]
                hi = jnp.where(swap, *ends[::-1]) if g == 3 else cur_ref[16 * g + 16, :, cols]
                below, here = halves(lo), halves(cur_ref[16 * g, :, cols])
                state = [[acc[side, h, i] for i in range(7)] for h in range(2)]
                for p in range(16):
                    above = halves(cur_ref[16 * g + p + 1, :, cols] if p < 15 else hi)
                    for h in range(2):
                        rows = pl.ds(pl.multiple_of(256 * g + 16 * p + 8 * h, 8), 8)
                        state[h] = sample(
                            below[h], here[h], above[h], dx[rows, lanes], dy[rows, lanes], state[h]
                        )
                    below, here = here, above
                for h in range(2):
                    for i in range(7):
                        acc[side, h, i] = state[h][i]

        for side in range(2):
            lanes = slice(LANES * side, LANES * side + LANES)
            for h in range(2):
                rows = slice(8 * h, 8 * h + 8)
                for i in range(3):
                    front_ref[half, i, rows, lanes] = acc[side, h, i]
                    back_ref[half, i, rows, lanes] = acc[side, h, 4 + i]
                front_ref[half, 3, rows, lanes] = 1.0 - acc[side, h, 3]


def march(vol, odd, za, zb, ya, yb, light, tf_color, tf_opacity):
    sx, sy = difference_matrices()
    steps = DEPTH // 2

    def follower(s):
        return jnp.minimum(2 * s + 2, DEPTH - 1)

    def block(width, place):
        return pl.BlockSpec((PLANES, ROWS, width), lambda s: (0, 0, place(s)))

    def matrix(place):
        return pl.BlockSpec((None, 512, WIDE), lambda s: (place(s), 0, 0))

    def edge(rows, width, place):
        return pl.BlockSpec((rows, width), lambda s: (0, place(s)))

    smem = pl.BlockSpec(memory_space=pltpu.SMEM)
    return pl.pallas_call(
        march_kernel,
        grid=(steps,),
        in_specs=[
            smem,
            smem,
            smem,
            smem,
            matrix(lambda s: 0),
            matrix(lambda s: 1),
            matrix(lambda s: jnp.where(s == steps - 1, 2, 1)),
            pl.BlockSpec((2, 2, 128, WIDE), lambda s: (0, 0, 0, 0)),
            block(LANES, lambda s: 0),
            block(2 * WIDE, lambda s: s),
            block(WIDE, follower),
            block(LANES, lambda s: jnp.minimum(4 * s + 6, 2 * DEPTH - 1)),
            edge(ROWS, 2 * WIDE, lambda s: s),
            edge(ROWS, 2 * WIDE, lambda s: s),
            edge(PLANES, 2 * WIDE, lambda s: s),
            edge(PLANES, 2 * WIDE, lambda s: s),
            edge(PLANES, WIDE, follower),
            edge(PLANES, WIDE, follower),
        ],
        out_specs=[
            pl.BlockSpec((2, n, ROWS, WIDE), lambda s: (s, 0, 0, 0)) for n in (4, 3)
        ],
        out_shape=[jax.ShapeDtypeStruct((DEPTH, n, ROWS, WIDE), f32) for n in (4, 3)],
        scratch_shapes=[pltpu.VMEM((PLANES * ROWS, WIDE), f32)] * 4
        + [pltpu.VMEM((2, 2, 7, 8, LANES), f32), pltpu.VMEM((104, LANES), f32)],
        compiler_params=pltpu.CompilerParams(vmem_limit_bytes=VMEM),
        cost_estimate=pl.CostEstimate(
            flops=400_000_000, bytes_accessed=24_000_000, transcendentals=4_000_000
        ),
        name="march",
    )(
        odd, light, tf_color, tf_opacity, sx, sx, sx, sy, vol, vol, vol, vol,
        za, zb, ya, yb, ya, yb,
    )


def edges_kernel(odd_ref, pick_ref, v_ref, za_ref, zb_ref, ya_ref, yb_ref):
    za_ref[...] = v_ref[(PLANES - 1) * (1 - odd_ref[1])]
    zb_ref[...] = v_ref[(PLANES - 1) * odd_ref[1]]
    width = v_ref.shape[2]
    for g in range(4):
        planes = slice(16 * g, 16 * g + 16)
        rows = v_ref[planes].reshape(256, width)
        rows = jnp.dot(pick_ref[odd_ref[0]], rows, preferred_element_type=f32).astype(bf16)
        ya_ref[planes, :] = rows[:16]
        yb_ref[planes, :] = rows[16:]


def edges(vol, odd):
    width = 2048
    choose = np.zeros((2, 32, 256), np.float32)
    for p in range(16):
        for o in range(2):
            choose[o, 16 * o + p, ROWS * p + ROWS - 1] = 1
            choose[o, 16 - 16 * o + p, ROWS * p] = 1
    return pl.pallas_call(
        edges_kernel,
        grid=(vol.shape[2] // width,),
        in_specs=[
            pl.BlockSpec(memory_space=pltpu.SMEM),
            pl.BlockSpec((2, 32, 256), lambda s: (0, 0, 0)),
            pl.BlockSpec((PLANES, ROWS, width), lambda s: (0, 0, s)),
        ],
        out_specs=[pl.BlockSpec((n, width), lambda s: (0, s)) for n in (ROWS, ROWS, PLANES, PLANES)],
        out_shape=[
            jax.ShapeDtypeStruct((n, vol.shape[2]), bf16) for n in (ROWS, ROWS, PLANES, PLANES)
        ],
        compiler_params=pltpu.CompilerParams(vmem_limit_bytes=58 * 1024 * 1024),
        name="edges",
    )(odd, jnp.asarray(choose, bf16), vol)


def front_kernel(bg_ref, prior_ref, s_ref, mapped_ref, lum_ref):
    total = jnp.zeros((8, LANES), f32)
    for c in range(2):
        cols = slice(LANES * c, LANES * c + LANES)
        front = [s_ref[0, i, :, cols] for i in range(3)]
        through = 1.0 - s_ref[0, 3, :, cols]
        for d in range(1, DEPTH):
            front = [front[i] + through * s_ref[d, i, :, cols] for i in range(3)]
            through = through - through * s_ref[d, 3, :, cols]
        front = [front[i] + through * bg_ref[i] for i in range(3)]
        lum = jnp.log(0.2126 * front[0] + 0.7152 * front[1] + 0.0722 * front[2] + LUMA_EPS)
        near = jnp.clip(lum, LOG_LOW, LOG_HIGH)
        term = near * jnp.maximum(0.0, 1.0 - jnp.abs(lum - near) * (1.0 / BIN_WIDTH))
        total = total + term[0:8] + term[8:16]
        for i in range(3):
            scaled = prior_ref[0] * front[i]
            mapped_ref[i, :, cols] = scaled / (1.0 + scaled)
    coarse = jnp.round(total * 64.0) * (1.0 / 64.0)
    lum_ref[...] = jnp.concatenate([coarse, total - coarse], axis=1)


def back_kernel(bg_ref, f_ref, s_ref, second_ref):
    for c in range(2):
        cols = slice(LANES * c, LANES * c + LANES)
        back = [s_ref[0, i, :, cols] for i in range(3)]
        through = 1.0 - f_ref[0, 3, :, cols]
        for d in range(1, DEPTH):
            keep = 1.0 - f_ref[d, 3, :, cols]
            back = [s_ref[d, i, :, cols] + keep * back[i] for i in range(3)]
            through = through * keep
        for i in range(3):
            second_ref[i, :, cols] = back[i] + through * bg_ref[i]


def finish_kernel(pixels, lum_ref, mapped_ref, second_ref, o_ref):
    total = jnp.sum(jnp.sum(lum_ref[...], axis=0), axis=(0, 1), keepdims=True)
    exposure = EXPOSURE_KEY * jnp.exp(-total / pixels)
    for i in range(3):
        o_ref[0, i] = mapped_ref[i]
        scaled = exposure * second_ref[i]
        o_ref[1, i] = scaled / (1.0 + scaled)


def swap(first, second, axis):
    count = lax.axis_size(axis)
    pairs = [(i, i ^ 1) for i in range(count)]
    others = [(i, i + 1 if i % 2 else i - 1) for i in range(1, count - 1)]
    return lax.ppermute(first, axis, pairs), lax.ppermute(second, axis, others)


def exchange(part, axis):
    return lax.all_to_all(part, axis, split_axis=0, concat_axis=0, tiled=True)


def local(volume, tf_color, tf_opacity, light, background, exposure_prior):
    odd = jnp.stack([lax.axis_index(axis) % 2 for axis in ("tile", "depth")])
    za, zb, ya, yb = edges(volume, odd)
    ya, yb = swap(ya, yb, "tile")
    za, zb = swap(za, zb, "depth")
    front, back = march(volume, odd, za, zb, ya, yb, light, tf_color, tf_opacity)
    smem = pl.BlockSpec(memory_space=pltpu.SMEM)
    vmem = pl.BlockSpec(memory_space=pltpu.VMEM)
    image = jax.ShapeDtypeStruct((3, ROWS, WIDE), f32)
    front = exchange(front.astype(f16), "depth").astype(f32)
    mapped, lum = pl.pallas_call(
        front_kernel,
        in_specs=[smem, smem, vmem],
        out_specs=[vmem] * 2,
        out_shape=[image, jax.ShapeDtypeStruct((8, WIDE), f32)],
        compiler_params=pltpu.CompilerParams(vmem_limit_bytes=SMALL),
        name="front",
    )(background, exposure_prior, front)
    lum = jnp.broadcast_to(jnp.pad(lum, ((0, 8), (0, 0))), (DEPTH, 1, ROWS, WIDE))
    back = exchange(jnp.concatenate([back, lum], axis=1).astype(f16), "depth")
    sums = jnp.sum(back[:, 3, :8].astype(f32), axis=0)
    sums = sums[:, :LANES] + sums[:, LANES:]
    sums = exchange(jnp.broadcast_to(sums, (lax.axis_size("tile"), 8, LANES)), "tile")
    second = pl.pallas_call(
        back_kernel,
        in_specs=[smem, vmem, vmem],
        out_specs=vmem,
        out_shape=image,
        compiler_params=pltpu.CompilerParams(vmem_limit_bytes=SMALL),
        name="back",
    )(background, front, back[:, :3].astype(f32))
    pixels = ROWS * lax.axis_size("tile") * volume.shape[2]
    return pl.pallas_call(
        functools.partial(finish_kernel, float(pixels)),
        in_specs=[vmem] * 3,
        out_specs=vmem,
        out_shape=jax.ShapeDtypeStruct((2, 3, ROWS, WIDE), f32),
        compiler_params=pltpu.CompilerParams(vmem_limit_bytes=SMALL),
        name="finish",
    )(sums, mapped, second)


def solution(mesh):
    placed = (P("depth", "tile", None), P(), P(), P(), P(), P())
    return jax.shard_map(
        local, mesh=mesh, in_specs=placed, out_specs=P(None, None, "tile", "depth"), check_vma=False
    )
```
